128 devices in a mesh: row: 8 (over x, core), col: 16 (over y, z).
Axes of the slice: x: 4, y: 4, z: 4, core: 2. Of those that a mesh axis runs over, the one named last changes fastest.
Arguments:
- a_tiles: bfloat16 [8, 16, 3, 8, 128, 128], P('row', 'col'), may hold values from -0.15625 to 0.15625
- a_rows: int32 [8, 16, 3, 8], P('row'), may hold values from 0 to 15, as said below
- a_cols: int32 [8, 16, 3, 8], P('row'), may hold values from 0 to 15, as said below
- p_tiles: bfloat16 [8, 3, 2, 16, 4, 128, 128], P('row', None, None, 'col'), may hold values from -6 to 6
- p_cols: int32 [8, 3, 2, 16, 4], P(None, None, None, 'col'), may hold values from 0 to 7, as said below
- owners: int32 [128, 1], P('row'), may hold values from 0 to 15; in each aligned block of 16 rows (0 to 15, 16 to 31, ...) at most 2 rows name the same one
Outputs:
- owned_rows: bfloat16 [256, 128, 128, 128], P(('row', 'col'))
The draws below stay inside these ranges and needn't reach their ends.
Inputs may be any that keep to these rules, and one draw needn't show every extreme that they name: For each row group and panel, the pairs (a_rows, a_cols) over all columns of devices and all 8 slots are distinct. `a_cols`: see a_rows. `p_cols`: the 4 entries of one tile row within one column group are distinct. `owners`: within each row group of 16 tile rows, no owner holds more than 2 of them.
All inputs are finite; a program needn't handle non-finite values.
Results may differ from the reference program's by a relative error of at most 0.001.
Values may be sent and summed in bfloat16 or wider, within the bound.
A program may use at most 128 MiB of HBM per device.

```python
import math
import jax
import jax.numpy as jnp
import numpy as np
from jax import lax

TILE = 128
SECTIONS = 3
BR = 16
KA = 8
BKL = 2
BC = 8
PJ = 4
MOST = 2
NBR = 128
BK = 16
NCB = 128
ROW_NNZ = 1536
N_ROW = 8
N_COL = 16


def slot_positions(key):
    groups = NBR // BR
    columns = NCB // BC
    keys = jax.random.split(key, groups * SECTIONS)
    perms = jax.vmap(lambda one_key: jax.random.permutation(one_key, BR * BK))(keys)
    chosen = perms[:, :columns * KA].reshape(groups, SECTIONS, columns, KA)
    return jnp.transpose(chosen, (0, 2, 1, 3)).astype(jnp.int32)


def draw_a_rows(key, part):
    positions = slot_positions(key)
    return (positions // BK).astype(jnp.int32)


def draw_a_cols(key, part):
    positions = slot_positions(key)
    return (positions % BK).astype(jnp.int32)


def draw_p_cols(key, part):
    key = jax.random.fold_in(key, 7)
    groups = NBR // BR
    columns = NCB // BC
    shape_full = (groups, SECTIONS, BKL, columns, BC)
    scores = jax.random.randint(key, shape_full, 0, 1 << 20) * BC + jnp.arange(BC, dtype=jnp.int32)
    order = jnp.argsort(scores, axis=-1, stable=True)
    return order[..., :PJ].astype(jnp.int32)


def level_of(rng, dims, shards, least, largest):
    def one(dim, parts):
        steps = jax.random.uniform(jax.random.fold_in(jax.random.fold_in(rng, 6), dim), (parts,), jnp.float32, least / len(shards), largest / len(shards))
        return jnp.repeat(jnp.exp(steps), dims[dim] // parts).reshape((-1,) + (1,) * (len(dims) - dim - 1))

    loudness = one(*shards[0])
    for cut in shards[1:]:
        loudness = loudness * one(*cut)
    return loudness


def assign_block(key, own, number, rows, count, top, bound, skew):
    ranking = jax.random.permutation(key, count)
    heavy_load, ordinary = portions_of(count, rows * top, bound, skew, True), portions_of(count, rows * top, bound, skew, False)
    places = jnp.arange(count)

    def named(sizes, offset_by):
        used = int((sizes > 0).sum())
        fixed = max(1, used // 4)
        moved = fixed + (places - fixed + offset_by * (used - fixed)) % max(1, count - fixed)
        return jnp.zeros((count,), jnp.int32).at[ranking[jnp.where(places < fixed, places, moved)]].set(jnp.asarray(sizes, jnp.int32))

    sizes = jnp.where(number % 4 == 0, named(heavy_load, number // 4), named(ordinary, number - number // 4 - 1))
    mixed = jax.random.permutation(jax.random.fold_in(own, 3), count)
    source_of, taker = mixed[0:count // 2 * 2:2], mixed[1:count // 2 * 2:2]
    margin = jnp.minimum(sizes[source_of] - 1, bound - sizes[taker]) // 2
    margin = jnp.where((source_of == ranking[0]) | (taker == ranking[0]) | (sizes[taker] == 0), 0, jnp.maximum(margin, 0))
    moved = jax.random.randint(jax.random.fold_in(own, 4), (count // 2,), 0, 1 << 20) % (margin + 1)
    sizes = sizes.at[source_of].add(-moved).at[taker].add(moved)
    items = jnp.searchsorted(jnp.cumsum(sizes), jnp.arange(rows * top), side="right").astype(jnp.int32)
    listing = items.reshape(top, rows).T
    listing = listing[jax.random.permutation(jax.random.fold_in(own, 1), rows)]
    offset_by = jax.random.randint(jax.random.fold_in(own, 2), (rows, 1), 0, top)
    return jnp.take_along_axis(listing, (jnp.arange(top)[None, :] + offset_by) % top, axis=1)


def portions_of(number_of, total, most, slope, full):
    weights = [(1 << 20) // math.isqrt(grade ** slope) + 1 for grade in range(1, number_of + 1)]
    largest = most if full else min(most, max(-(-total // number_of), total * weights[0] // sum(weights)))
    least = 1 if total - largest >= number_of - 1 else 0
    given, spare = [largest] + [least] * (number_of - 1), total - largest - least * (number_of - 1)
    while spare > 0:
        candidates = [i for i in range(1, number_of) if given[i] < largest] or [i for i in range(1, number_of) if given[i] < most]
        mass, budget = sum([weights[i] for i in candidates]), spare
        for i in candidates:
            addition = min(most - given[i], max(1, budget * weights[i] // mass), spare)
            given[i] = given[i] + addition
            spare = spare - addition
    return np.array(given)


def centred(stream_key, extent, width, bound, pieces=(), kind=jnp.bfloat16):
    array = jax.random.normal(stream_key, extent, jnp.float32) * width
    if len(pieces) > 0:
        array = level_of(stream_key, extent, pieces, -0.22, 0.18) * array
    return jnp.clip(array, min=-bound, max=bound).astype(kind)


def setup_inputs(seed: int = 0) -> dict:
    key_of = jax.random.split(jax.random.key(seed), 7)
    a_tiles = centred(key_of[0], (N_ROW, N_COL, SECTIONS, KA, TILE, TILE), ROW_NNZ ** -0.5, 0.15625, ((0, 8), (1, 16)))
    a_rows = draw_a_rows(jax.random.fold_in(key_of[6], 71), 0)
    a_cols = draw_a_cols(jax.random.fold_in(key_of[6], 71), 0)
    p_tiles = centred(key_of[3], (N_ROW, SECTIONS, BKL, N_COL, PJ, TILE, TILE), 1.0, 6.0, ((0, 8), (3, 16)))
    p_cols = draw_p_cols(jax.random.fold_in(key_of[6], 71), 0)
    owners_keys = jax.random.split(jax.random.fold_in(key_of[5], 1), NBR // BR)
    owners_turns = jax.random.permutation(jax.random.fold_in(key_of[5], 3), NBR // BR)
    owners = jax.vmap(lambda own, number: assign_block(jax.random.fold_in(key_of[5], 2), own, number, BR, N_COL, 1, MOST, 2))(owners_keys, owners_turns).reshape((NBR, 1))
    return dict(a_tiles=a_tiles, a_rows=a_rows, a_cols=a_cols, p_tiles=p_tiles, p_cols=p_cols, owners=owners)


def slot_table(owner_list, column_count, slot_count):
    length = owner_list.shape[0]
    index_line = jnp.arange(length, dtype=jnp.int32)
    same_owner = owner_list[:, None] == owner_list[None, :]
    earlier = index_line[None, :] < index_line[:, None]
    rank_line = jnp.sum((same_owner & earlier).astype(jnp.int32), axis=1)
    owner_ids = jnp.arange(column_count, dtype=jnp.int32)
    slot_ids = jnp.arange(slot_count, dtype=jnp.int32)
    matches = (owner_list[None, None, :] == owner_ids[:, None, None]) & (rank_line[None, None, :] == slot_ids[None, :, None])
    source = jnp.sum(jnp.where(matches, index_line[None, None, :], 0), axis=2).astype(jnp.int32)
    valid = jnp.any(matches, axis=2)
    return source, valid


def reference(a_tiles, a_rows, a_cols, p_tiles, p_cols, owners):
    groups = NBR // BR
    columns = NCB // BC
    owner_groups = owners.reshape(groups, BR)
    col_base = (jnp.arange(columns, dtype=jnp.int32) * BC)[None, :, None]

    def one_group(inputs):
        tiles_g, rows_g, kcols_g, owner_list = inputs
        product = jnp.zeros((BR, NCB, TILE, TILE), jnp.float32)
        for section_idx in range(SECTIONS):
            panel = p_tiles[:, section_idx].reshape(BK, columns, PJ, TILE, TILE).astype(jnp.float32)
            targets = col_base + p_cols[:, section_idx].reshape(BK, columns, PJ)
            tiles_s = tiles_g[:, section_idx].reshape(columns * KA, TILE, TILE)
            rows_s = rows_g[:, section_idx].reshape(columns * KA)
            kblk_s = kcols_g[:, section_idx].reshape(columns * KA)

            def add_tile(running, item):
                one_tile, tile_row, k_block = item
                prow = panel[k_block]
                term = jnp.einsum('ab,cpbd->cpad', one_tile.astype(jnp.float32), prow)
                return running.at[tile_row, targets[k_block]].add(term), None

            product, _ = lax.scan(add_tile, product, (tiles_s, rows_s, kblk_s))
        rounded = product.astype(jnp.bfloat16)
        source, valid = slot_table(owner_list, columns, MOST)
        picked = rounded[source]
        return jnp.where(valid[:, :, None, None, None], picked, jnp.zeros_like(picked))

    stacked = lax.map(one_group, (a_tiles, a_rows, a_cols, owner_groups))
    return stacked.reshape(groups * columns * MOST, NCB, TILE, TILE)
```

```python
import functools

import jax
import jax.numpy as jnp
from jax import lax
from jax.experimental import pallas as pl
from jax.experimental.pallas import tpu as pltpu
from jax.sharding import PartitionSpec as P

SECTIONS = 3
BR = 16
BK = 16
BC = 8
KA = 8
PJ = 4
MOST = 2
TILE = 128
N_COL = 16
RING = 4
MESH = pl.DeviceIdType.MESH
A_SLOTS = N_COL * KA
P_SLOTS = BK * PJ
P_BASE = SECTIONS * BR * BK
O_BASE = P_BASE + SECTIONS * BK * BC
WIDE = 2
CHUNKS = BC // WIDE
MB = 512

ORDER = (
    (0, 1), (1, 0), (2, 2), (0, 3), (3, 0), (1, 1), (3, 3), (2, 0),
    (0, 2), (1, 3), (3, 1), (1, 2), (2, 1), (3, 2), (2, 3),
)
N_COPIES = SECTIONS * (44 + 7) + CHUNKS * 15


def kernel(tbl, a_ref, p_ref, out_ref, ar0, ar1, ar2, pr0, pr1, pr2, a_dense, p_dense, acc, rounded, staged, ssem, rsem, lsem):
    a_raw, p_raw = (ar0, ar1, ar2), (pr0, pr1, pr2)
    row, col = lax.axis_index("row"), lax.axis_index("col")
    x, core = row // 2, row % 2
    y, z = col // RING, col % RING

    def yz(dy, dz):
        return ((y + dy) % RING) * RING + (z + dz) % RING

    def xc(dx, dc):
        return ((x + dx) % RING) * 2 + (core + dc) % 2

    for s in range(SECTIONS):
        a_raw[s][A_SLOTS] = jnp.zeros((TILE, TILE), jnp.bfloat16)
        p_raw[s][P_SLOTS] = jnp.zeros((TILE, TILE), jnp.bfloat16)
    rounded[BR] = jnp.zeros((WIDE, TILE, TILE), jnp.bfloat16)

    barrier = pltpu.get_barrier_semaphore()
    peers = [{"col": yz(dy, dz)} for dy, dz in ORDER]
    peers += [{"row": xc(dx, 0)} for dx in (1, 3, 2)] + [{"row": xc(0, 1)}]
    for peer in peers:
        pl.semaphore_signal(barrier, inc=1, device_id=peer, device_id_type=MESH)
    pl.semaphore_wait(barrier, len(peers))

    copies = []
    local = []

    def send(src, dst, peer):
        i = len(copies)
        copy = pltpu.make_async_remote_copy(
            src_ref=src, dst_ref=dst, send_sem=ssem.at[i], recv_sem=rsem.at[i], device_id=peer, device_id_type=MESH
        )
        copy.start()
        copies.append(copy)
        return copy

    def keep(src, dst):
        copy = pltpu.make_async_copy(src, dst, lsem.at[len(local)])
        copy.start()
        local.append(copy)
        return copy

    def a_part(s, dy, dz, lo, n):
        return a_raw[s].at[pl.ds(yz(dy, dz) * KA + lo, n)]

    def fwd_a(s, dy, dz, lo, n, ty, tz):
        part = a_part(s, dy, dz, lo, n)
        return send(part, part, {"col": yz(ty, tz)})

    half = KA // 2
    quarter = KA // 4
    got = {}

    def pos(first, d1, d2):
        return (d2, d1) if first == 0 else (d1, d2)

    def stage_own(s):
        for n1 in (1, 3):
            for first in (0, 1):
                for along in (0, 1):
                    to = pos(first, n1, 0) if along == 0 else pos(first, 0, n1)
                    lo = first * half
                    got[s, first, "own", along, n1] = send(
                        a_ref.at[s, pl.ds(lo, half)], a_part(s, 0, 0, lo, half), {"col": yz(*to)}
                    )
        got[s, "kept"] = keep(a_ref.at[s], a_part(s, 0, 0, 0, KA))

    def stage_near(s):
        for n1 in (1, 3):
            for first in (0, 1):
                got[s, first, "own", 0, n1].wait_recv()
                dy, dz = pos(first, -n1, 0)
                lo = first * half
                q = lo + (0 if n1 == 1 else quarter)
                got[s, first, "far", n1] = fwd_a(s, dy, dz, q, quarter, *pos(first, n1, 0))
                for n2 in (1, 3):
                    got[s, first, "turn", n1, n2] = fwd_a(s, dy, dz, lo, half, *pos(first, 0, n2))

    def stage_far(s):
        for n1 in (1, 3):
            for first in (0, 1):
                got[s, first, "far", n1].wait_recv()
                dy, dz = pos(first, 2, 0)
                q = first * half + (0 if n1 == 1 else quarter)
                for n2 in (1, 3):
                    got[s, first, "farturn", n1, n2] = fwd_a(s, dy, dz, q, quarter, *pos(first, 0, n2))

    def stage_second(s, part):
        for n2 in (1, 3):
            for first in (0, 1):
                q = first * half + (0 if n2 == 1 else quarter)
                if part == 0:
                    got[s, first, "own", 1, n2].wait_recv()
                    dy, dz = pos(first, 0, -n2)
                    got[s, first, "end", 0, n2] = fwd_a(s, dy, dz, q, quarter, *pos(first, 0, n2))
                elif part == 1:
                    for n1 in (1, 3):
                        got[s, first, "turn", n1, n2].wait_recv()
                        dy, dz = pos(first, -n1, -n2)
                        got[s, first, "end", n1, n2] = fwd_a(s, dy, dz, q, quarter, *pos(first, 0, n2))
                else:
                    for n1 in (1, 3):
                        got[s, first, "farturn", n1, n2].wait_recv()
                        if n1 == n2:
                            dy, dz = pos(first, 2, -n2)
                            got[s, first, "end", 2, n2] = fwd_a(s, dy, dz, q, quarter, *pos(first, 0, n2))

    def stage_end(s):
        for n2 in (1, 3):
            for first in (0, 1):
                for n1 in (0, 1, 3, 2):
                    got[s, first, "end", n1, n2].wait_recv()
        got[s, "kept"].wait()

    def p_part(s, dx, dc):
        return p_raw[s].at[pl.ds(xc(dx, dc) * 2 * PJ, 2 * PJ)]

    def p_own(s):
        for dx in (1, 3, 2):
            got[s, "p", dx] = send(p_ref.at[s], p_part(s, 0, 0), {"row": xc(dx, 0)})
        got[s, "p", 0] = send(p_ref.at[s], p_part(s, 0, 0), {"row": xc(0, 1)})
        got[s, "pkept"] = keep(p_ref.at[s], p_part(s, 0, 0))

    def p_share(s):
        for dx in (1, 3, 2):
            got[s, "p", dx].wait_recv()
            got[s, "ps", dx] = send(p_part(s, -dx, 0), p_part(s, -dx, 0), {"row": xc(0, 1)})

    def p_end(s):
        got[s, "p", 0].wait_recv()
        for dx in (1, 3, 2):
            got[s, "ps", dx].wait_recv()
        got[s, "pkept"].wait()

    def place_p(s):
        @pl.loop(0, BK)
        def _(k):
            for c in range(BC):
                p_dense[pl.ds(pl.multiple_of(k * TILE, TILE), TILE), c * TILE : (c + 1) * TILE] = p_raw[s][
                    tbl[P_BASE + s * BK * BC + k * BC + c]
                ]

    def place_a(s):
        @pl.loop(0, BR)
        def _(r):
            for k in range(BK):
                a_dense[pl.ds(pl.multiple_of(r * TILE, TILE), TILE), k * TILE : (k + 1) * TILE] = a_raw[s][
                    tbl[s * BR * BK + r * BK + k]
                ]

    def part_dot(mb, nb):
        rows = pl.ds(pl.multiple_of(mb * MB, MB), MB)
        return jnp.dot(
            a_dense[rows, :], p_dense[:, nb * WIDE * TILE : (nb + 1) * WIDE * TILE], preferred_element_type=jnp.float32
        )

    def dots(s, nb):
        @pl.loop(0, BR * TILE // MB)
        def _(mb):
            rows = pl.ds(pl.multiple_of(mb * MB, MB), MB)
            value = part_dot(mb, nb)
            if s == 0:
                acc[nb, rows, :] = value
            else:
                acc[nb, rows, :] += value

    def finish(nb):
        @pl.loop(0, BR * TILE // MB)
        def _(mb):
            rows = pl.ds(pl.multiple_of(mb * MB, MB), MB)
            value = (acc[nb, rows, :] + part_dot(mb, nb)).astype(jnp.bfloat16)
            for i in range(MB // TILE):
                for j in range(WIDE):
                    rounded[mb * (MB // TILE) + i, j] = value[i * TILE : (i + 1) * TILE, j * TILE : (j + 1) * TILE]

        @pl.loop(0, N_COL)
        def _(o):
            for q in range(MOST):
                staged[nb, o, q] = rounded[tbl[O_BASE + o * MOST + q]]

        where = out_ref.at[:, pl.ds(col * BC + nb * WIDE, WIDE)]
        for dy, dz in ORDER:
            got["out", nb, dy, dz] = send(staged.at[nb, yz(dy, dz)], where, {"col": yz(dy, dz)})
        keep(staged.at[nb, col], where)

    stage_own(0)
    p_own(0)
    stage_own(1)
    stage_near(0)
    stage_far(0)
    stage_second(0, 0)
    p_own(1)
    p_own(2)
    stage_second(0, 1)
    stage_second(0, 2)
    stage_own(2)
    stage_near(1)
    p_share(0)
    stage_far(1)
    stage_end(0)
    p_end(0)
    place_p(0)
    place_a(0)
    stage_second(1, 0)
    dots(0, 0)
    stage_second(1, 1)
    dots(0, 1)
    stage_second(1, 2)
    stage_near(2)
    dots(0, 2)
    p_share(1)
    stage_far(2)
    dots(0, 3)
    stage_end(1)
    p_share(2)
    p_end(1)
    stage_second(2, 0)
    place_p(1)
    place_a(1)
    stage_second(2, 1)
    dots(1, 0)
    dots(1, 1)
    stage_second(2, 2)
    dots(1, 2)
    dots(1, 3)
    p_end(2)
    place_p(2)
    stage_end(2)
    place_a(2)
    for nb in range(CHUNKS):
        finish(nb)
    for nb in range(CHUNKS):
        for dy, dz in ORDER:
            got["out", nb, dy, dz].wait_recv()
    for copy in copies:
        copy.wait_send()
    for copy in local[2 * SECTIONS :]:
        copy.wait()


def tables(a_rows, a_cols, p_cols, owners):
    codes = jnp.transpose(a_rows[0] * BK + a_cols[0], (1, 0, 2)).reshape(SECTIONS, A_SLOTS)
    spots = jnp.arange(BR * BK, dtype=jnp.int32)
    slots = jnp.arange(A_SLOTS, dtype=jnp.int32)
    a_tbl = jnp.min(jnp.where(codes[:, None, :] == spots[None, :, None], slots[None, None, :], A_SLOTS), axis=2)
    cols = jnp.transpose(p_cols[:, :, :, 0], (1, 0, 2, 3)).reshape(SECTIONS, P_SLOTS)
    group = jnp.arange(BK * BC, dtype=jnp.int32)
    slots = jnp.arange(P_SLOTS, dtype=jnp.int32)
    place = (slots // PJ)[None, :] * BC + cols
    p_tbl = jnp.min(jnp.where(place[:, None, :] == group[None, :, None], slots[None, None, :], P_SLOTS), axis=2)
    owner = owners[:, 0]
    line = jnp.arange(BR, dtype=jnp.int32)
    rank = jnp.sum(((owner[:, None] == owner[None, :]) & (line[None, :] < line[:, None])).astype(jnp.int32), axis=1)
    spot = owner * MOST + rank
    outs = jnp.arange(N_COL * MOST, dtype=jnp.int32)
    o_tbl = jnp.min(jnp.where(spot[None, :] == outs[:, None], line[None, :], BR), axis=1)
    return jnp.concatenate([a_tbl.reshape(-1), p_tbl.reshape(-1), o_tbl]).astype(jnp.int32)


def body(a_tiles, a_rows, a_cols, p_tiles, p_cols, owners):
    tbl = tables(a_rows, a_cols, p_cols, owners)
    a = a_tiles.reshape(SECTIONS, KA, TILE, TILE)
    p = p_tiles.reshape(SECTIONS, 2 * PJ, TILE, TILE)
    bf = jnp.bfloat16
    return pl.pallas_call(
        kernel,
        name="block_product",
        out_shape=jax.ShapeDtypeStruct((MOST, N_COL * BC, TILE, TILE), bf),
        in_specs=[
            pl.BlockSpec(memory_space=pltpu.SMEM),
            pl.BlockSpec(memory_space=pl.ANY),
            pl.BlockSpec(memory_space=pl.ANY),
        ],
        out_specs=pl.BlockSpec(memory_space=pl.ANY),
        scratch_shapes=[pltpu.VMEM((A_SLOTS + 1, TILE, TILE), bf)] * SECTIONS
        + [pltpu.VMEM((P_SLOTS + 1, TILE, TILE), bf)] * SECTIONS
        + [
            pltpu.VMEM((BR * TILE, BK * TILE), bf),
            pltpu.VMEM((BK * TILE, BC * TILE), bf),
            pltpu.VMEM((CHUNKS, BR * TILE, WIDE * TILE), jnp.float32),
            pltpu.VMEM((BR + 1, WIDE, TILE, TILE), bf),
            pltpu.VMEM((CHUNKS, N_COL, MOST, WIDE, TILE, TILE), bf),
            pltpu.SemaphoreType.DMA((N_COPIES,)),
            pltpu.SemaphoreType.DMA((N_COPIES,)),
            pltpu.SemaphoreType.DMA((2 * SECTIONS + CHUNKS,)),
        ],
        compiler_params=pltpu.CompilerParams(collective_id=0, has_side_effects=True, vmem_limit_bytes=60 << 20),
        cost_estimate=pl.CostEstimate(flops=25_769_803_776, bytes_accessed=20_000_000, transcendentals=0),
    )(tbl, a, p)


def solution(mesh):
    placed = (
        P("row", "col", None, None, None, None),
        P("row", None, None, None),
        P("row", None, None, None),
        P("row", None, None, "col", None, None, None),
        P(None, None, None, "col", None),
        P("row", None),
    )
    return jax.shard_map(
        body,
        mesh=mesh,
        in_specs=placed,
        out_specs=P(("row", "col"), None, None, None),
        check_vma=False,
    )
```

```python
import functools

import jax
import jax.numpy as jnp
from jax import lax
from jax.experimental import pallas as pl
from jax.experimental.pallas import tpu as pltpu
from jax.sharding import PartitionSpec as P

SECTIONS = 3
BR = 16
BK = 16
BC = 8
KA = 8
PJ = 4
MOST = 2
TILE = 128
N_COL = 16
RING = 4
MESH = pl.DeviceIdType.MESH
A_SLOTS = N_COL * KA
P_SLOTS = BK * PJ
WIDE = 2
CHUNKS = BC // WIDE
MB = 512
PIECES = 4

ORDER = (
    (0, 1), (1, 0), (2, 2), (0, 3), (3, 0), (1, 1), (3, 3), (2, 0),
    (0, 2), (1, 3), (3, 1), (1, 2), (2, 1), (3, 2), (2, 3),
)
N_COPIES = SECTIONS * (44 + 7) + CHUNKS * 15


def kernel(
    a_rows, a_cols, p_cols, owners, a_ref, p_ref, out_ref,
    ar0, ar1, ar2, pr0, pr1, pr2, a_dense, p_dense, acc, rounded, staged, found, tbl, ssem, rsem, lsem, tsem,
):
    a_raw, p_raw = (ar0, ar1, ar2), (pr0, pr1, pr2)
    row, col = lax.axis_index("row"), lax.axis_index("col")
    x, core = row // 2, row % 2
    y, z = col // RING, col % RING

    def yz(dy, dz):
        return ((y + dy) % RING) * RING + (z + dz) % RING

    def xc(dx, dc):
        return ((x + dx) % RING) * 2 + (core + dc) % 2

    for s in range(SECTIONS):
        a_raw[s][A_SLOTS] = jnp.zeros((TILE, TILE), jnp.bfloat16)
        p_raw[s][P_SLOTS] = jnp.zeros((TILE, TILE), jnp.bfloat16)
    rounded[BR] = jnp.zeros((WIDE, TILE, TILE), jnp.bfloat16)

    barrier = pltpu.get_barrier_semaphore()
    peers = [{"col": yz(dy, dz)} for dy, dz in ORDER]
    peers += [{"row": xc(dx, 0)} for dx in (1, 3, 2)] + [{"row": xc(0, 1)}]
    for peer in peers:
        pl.semaphore_signal(barrier, inc=1, device_id=peer, device_id_type=MESH)
    pl.semaphore_wait(barrier, len(peers))

    copies = []
    local = []

    def send(src, dst, peer):
        i = len(copies)
        copy = pltpu.make_async_remote_copy(
            src_ref=src, dst_ref=dst, send_sem=ssem.at[i], recv_sem=rsem.at[i], device_id=peer, device_id_type=MESH
        )
        copy.start()
        copies.append(copy)
        return copy

    def keep(src, dst):
        copy = pltpu.make_async_copy(src, dst, lsem.at[len(local)])
        copy.start()
        local.append(copy)
        return copy

    def a_part(s, dy, dz, lo, n):
        return a_raw[s].at[pl.ds(yz(dy, dz) * KA + lo, n)]

    def fwd_a(s, dy, dz, lo, n, ty, tz):
        part = a_part(s, dy, dz, lo, n)
        return send(part, part, {"col": yz(ty, tz)})

    half = KA // 2
    quarter = KA // 4
    got = {}

    def pos(first, d1, d2):
        return (d2, d1) if first == 0 else (d1, d2)

    def stage_own(s):
        for n1 in (1, 3):
            for first in (0, 1):
                for along in (0, 1):
                    to = pos(first, n1, 0) if along == 0 else pos(first, 0, n1)
                    lo = first * half
                    got[s, first, "own", along, n1] = send(
                        a_ref.at[s, pl.ds(lo, half)], a_part(s, 0, 0, lo, half), {"col": yz(*to)}
                    )
        got[s, "kept"] = keep(a_ref.at[s], a_part(s, 0, 0, 0, KA))

    def stage_near(s):
        for n1 in (1, 3):
            for first in (0, 1):
                got[s, first, "own", 0, n1].wait_recv()
                dy, dz = pos(first, -n1, 0)
                lo = first * half
                q = lo + (0 if n1 == 1 else quarter)
                got[s, first, "far", n1] = fwd_a(s, dy, dz, q, quarter, *pos(first, n1, 0))
                for n2 in (1, 3):
                    got[s, first, "turn", n1, n2] = fwd_a(s, dy, dz, lo, half, *pos(first, 0, n2))

    def stage_far(s):
        for n1 in (1, 3):
            for first in (0, 1):
                got[s, first, "far", n1].wait_recv()
                dy, dz = pos(first, 2, 0)
                q = first * half + (0 if n1 == 1 else quarter)
                for n2 in (1, 3):
                    got[s, first, "farturn", n1, n2] = fwd_a(s, dy, dz, q, quarter, *pos(first, 0, n2))

    def stage_second(s, part):
        for n2 in (1, 3):
            for first in (0, 1):
                q = first * half + (0 if n2 == 1 else quarter)
                if part == 0:
                    got[s, first, "own", 1, n2].wait_recv()
                    dy, dz = pos(first, 0, -n2)
                    got[s, first, "end", 0, n2] = fwd_a(s, dy, dz, q, quarter, *pos(first, 0, n2))
                elif part == 1:
                    for n1 in (1, 3):
                        got[s, first, "turn", n1, n2].wait_recv()
                        dy, dz = pos(first, -n1, -n2)
                        got[s, first, "end", n1, n2] = fwd_a(s, dy, dz, q, quarter, *pos(first, 0, n2))
                else:
                    for n1 in (1, 3):
                        got[s, first, "farturn", n1, n2].wait_recv()
                        if n1 == n2:
                            dy, dz = pos(first, 2, -n2)
                            got[s, first, "end", 2, n2] = fwd_a(s, dy, dz, q, quarter, *pos(first, 0, n2))

    def stage_end(s):
        for n2 in (1, 3):
            for first in (0, 1):
                for n1 in (0, 1, 3, 2):
                    got[s, first, "end", n1, n2].wait_recv()
        got[s, "kept"].wait()

    def p_part(s, dx, dc):
        return p_raw[s].at[pl.ds(xc(dx, dc) * 2 * PJ, 2 * PJ)]

    def p_own(s):
        for dx in (1, 3, 2):
            got[s, "p", dx] = send(p_ref.at[s], p_part(s, 0, 0), {"row": xc(dx, 0)})
        got[s, "p", 0] = send(p_ref.at[s], p_part(s, 0, 0), {"row": xc(0, 1)})
        got[s, "pkept"] = keep(p_ref.at[s], p_part(s, 0, 0))

    def p_share(s):
        for dx in (1, 3, 2):
            got[s, "p", dx].wait_recv()
            got[s, "ps", dx] = send(p_part(s, -dx, 0), p_part(s, -dx, 0), {"row": xc(0, 1)})

    def p_end(s):
        got[s, "p", 0].wait_recv()
        for dx in (1, 3, 2):
            got[s, "ps", dx].wait_recv()
        got[s, "pkept"].wait()

    def find():
        def iota(shape, dim):
            return lax.broadcasted_iota(jnp.int32, shape, dim)

        def column(line):
            n = line.shape[1]
            return jnp.sum(jnp.where(iota((n, n), 0) == iota((n, n), 1), line, 0), axis=1, keepdims=True)

        spots = iota((N_COL, BR * BK), 1)
        first = iota((N_COL, BR * BK), 0) * KA
        for s in range(SECTIONS):
            codes = a_rows[s] * BK + a_cols[s]
            best = jnp.full((N_COL, BR * BK), A_SLOTS, jnp.int32)
            for t in range(KA):
                best = jnp.minimum(best, jnp.where(column(codes[t : t + 1]) == spots, first + t, A_SLOTS))
            found[s : s + 1, :] = jnp.min(best, axis=0, keepdims=True)
        n_row = BK // 2
        spots = iota((n_row, BK * BC), 1)
        group = iota((n_row, BK * BC), 0)
        for s in range(SECTIONS):
            best = jnp.full((n_row, BK * BC), P_SLOTS, jnp.int32)
            for m in range(2):
                cols = p_cols[s, m]
                k = group * 2 + m
                for j in range(PJ):
                    best = jnp.minimum(best, jnp.where(k * BC + column(cols[j : j + 1]) == spots, k * PJ + j, P_SLOTS))
            found[SECTIONS + s : SECTIONS + s + 1, : BK * BC] = jnp.min(best, axis=0, keepdims=True)
        line = iota((BR, TILE), 0)
        spots = iota((BR, TILE), 1)
        named = column(owners[...]) == spots // MOST
        low = jnp.min(jnp.where(named, line, BR), axis=0, keepdims=True)
        high = jnp.max(jnp.where(named, line, -1), axis=0, keepdims=True)
        second = jnp.where(high > low, high, BR)
        slot = iota((1, TILE), 1) % MOST
        found[2 * SECTIONS : 2 * SECTIONS + 1, :TILE] = jnp.where(slot == 0, low, second)
        copy = pltpu.make_async_copy(found, tbl, tsem)
        copy.start()
        copy.wait()

    def place_p(s):
        @pl.loop(0, BK)
        def _(k):
            for c in range(BC):
                p_dense[pl.ds(pl.multiple_of(k * TILE, TILE), TILE), c * TILE : (c + 1) * TILE] = p_raw[s][
                    tbl[SECTIONS + s, k * BC + c]
                ]

    def place_a(s):
        @pl.loop(0, BR)
        def _(r):
            for k in range(BK):
                a_dense[pl.ds(pl.multiple_of(r * TILE, TILE), TILE), k * TILE : (k + 1) * TILE] = a_raw[s][
                    tbl[s, r * BK + k]
                ]

    def part_dot(mb, nb):
        rows = pl.ds(pl.multiple_of(mb * MB, MB), MB)
        return jnp.dot(
            a_dense[rows, :], p_dense[:, nb * WIDE * TILE : (nb + 1) * WIDE * TILE], preferred_element_type=jnp.float32
        )

    def dots(s, nb):
        @pl.loop(0, BR * TILE // MB)
        def _(mb):
            rows = pl.ds(pl.multiple_of(mb * MB, MB), MB)
            value = part_dot(mb, nb)
            if s == 0:
                acc[nb, rows, :] = value
            else:
                acc[nb, rows, :] += value

    def finish(nb):
        @pl.loop(0, BR * TILE // MB)
        def _(mb):
            rows = pl.ds(pl.multiple_of(mb * MB, MB), MB)
            value = (acc[nb, rows, :] + part_dot(mb, nb)).astype(jnp.bfloat16)
            for i in range(MB // TILE):
                for j in range(WIDE):
                    rounded[mb * (MB // TILE) + i, j] = value[i * TILE : (i + 1) * TILE, j * TILE : (j + 1) * TILE]

        @pl.loop(0, N_COL)
        def _(o):
            for q in range(MOST):
                staged[nb, o, q] = rounded[tbl[2 * SECTIONS, o * MOST + q]]

        where = out_ref.at[:, pl.ds(col * BC + nb * WIDE, WIDE)]
        for dy, dz in ORDER:
            got["out", nb, dy, dz] = send(staged.at[nb, yz(dy, dz)], where, {"col": yz(dy, dz)})
        keep(staged.at[nb, col], where)

    stage_own(0)
    p_own(0)
    stage_own(1)
    find()
    stage_near(0)
    stage_far(0)
    stage_second(0, 0)
    p_own(1)
    p_own(2)
    stage_second(0, 1)
    stage_second(0, 2)
    stage_own(2)
    stage_near(1)
    p_share(0)
    stage_far(1)
    stage_end(0)
    p_end(0)
    place_p(0)
    place_a(0)
    stage_second(1, 0)
    dots(0, 0)
    stage_second(1, 1)
    dots(0, 1)
    stage_second(1, 2)
    stage_near(2)
    dots(0, 2)
    p_share(1)
    stage_far(2)
    dots(0, 3)
    stage_end(1)
    p_share(2)
    p_end(1)
    stage_second(2, 0)
    place_p(1)
    place_a(1)
    stage_second(2, 1)
    dots(1, 0)
    dots(1, 1)
    stage_second(2, 2)
    dots(1, 2)
    dots(1, 3)
    p_end(2)
    place_p(2)
    stage_end(2)
    place_a(2)
    for nb in range(CHUNKS):
        finish(nb)
    for nb in range(CHUNKS):
        for dy, dz in ORDER:
            got["out", nb, dy, dz].wait_recv()
    for copy in copies:
        copy.wait_send()
    for copy in local[2 * SECTIONS :]:
        copy.wait()


def settle(held, out_ref, sems):
    n = N_COL * BC // PIECES
    copies = []
    for q in range(MOST):
        for i in range(PIECES):
            part = (q, pl.ds(i * n, n))
            copies.append(pltpu.make_async_copy(held.at[part], out_ref.at[part], sems.at[q * PIECES + i]))
            copies[-1].start()
    for copy in copies:
        copy.wait()


def body(a_tiles, a_rows, a_cols, p_tiles, p_cols, owners):
    a = a_tiles.reshape(SECTIONS, KA, TILE, TILE)
    p = p_tiles.reshape(SECTIONS, 2 * PJ, TILE, TILE)
    bf = jnp.bfloat16
    vmem = pl.BlockSpec(memory_space=pltpu.VMEM)
    hbm = pl.BlockSpec(memory_space=pl.ANY)
    shape = (MOST, N_COL * BC, TILE, TILE)
    held = pl.pallas_call(
        kernel,
        name="block_product",
        out_shape=pltpu.VMEM(shape, bf),
        in_specs=[vmem] * 4 + [hbm] * 2,
        out_specs=vmem,
        scratch_shapes=[pltpu.VMEM((A_SLOTS + 1, TILE, TILE), bf)] * SECTIONS
        + [pltpu.VMEM((P_SLOTS + 1, TILE, TILE), bf)] * SECTIONS
        + [
            pltpu.VMEM((BR * TILE, BK * TILE), bf),
            pltpu.VMEM((BK * TILE, BC * TILE), bf),
            pltpu.VMEM((CHUNKS, BR * TILE, WIDE * TILE), jnp.float32),
            pltpu.VMEM((BR + 1, WIDE, TILE, TILE), bf),
            pltpu.VMEM((CHUNKS, N_COL, MOST, WIDE, TILE, TILE), bf),
            pltpu.VMEM((8, BR * BK), jnp.int32),
            pltpu.SMEM((8, BR * BK), jnp.int32),
            pltpu.SemaphoreType.DMA((N_COPIES,)),
            pltpu.SemaphoreType.DMA((N_COPIES,)),
            pltpu.SemaphoreType.DMA((2 * SECTIONS + CHUNKS,)),
            pltpu.SemaphoreType.DMA,
        ],
        compiler_params=pltpu.CompilerParams(collective_id=0, has_side_effects=True, vmem_limit_bytes=52 << 20),
        cost_estimate=pl.CostEstimate(flops=25_769_803_776, bytes_accessed=20_000_000, transcendentals=0),
    )(
        jnp.transpose(a_rows[0], (1, 2, 0)),
        jnp.transpose(a_cols[0], (1, 2, 0)),
        jnp.transpose(p_cols[:, :, :, 0], (1, 2, 3, 0)),
        owners.reshape(1, BR),
        a,
        p,
    )
    return pl.pallas_call(
        settle,
        name="settle",
        out_shape=jax.ShapeDtypeStruct(shape, bf),
        in_specs=[vmem],
        out_specs=hbm,
        scratch_shapes=[pltpu.SemaphoreType.DMA((MOST * PIECES,))],
        compiler_params=pltpu.CompilerParams(vmem_limit_bytes=2 << 20),
    )(held)


def solution(mesh):
    placed = (
        P("row", "col", None, None, None, None),
        P("row", None, None, None),
        P("row", None, None, None),
        P("row", None, None, "col", None, None, None),
        P(None, None, None, "col", None),
        P("row", None),
    )
    return jax.shard_map(
        body,
        mesh=mesh,
        in_specs=placed,
        out_specs=P(("row", "col"), None, None, None),
        check_vma=False,
    )
```

```python
import functools

import jax
import jax.numpy as jnp
from jax import lax
from jax.experimental import pallas as pl
from jax.experimental.pallas import tpu as pltpu
from jax.sharding import PartitionSpec as P

SECTIONS = 3
BR = 16
BK = 16
BC = 8
KA = 8
PJ = 4
MOST = 2
TILE = 128
N_COL = 16
RING = 4
MESH = pl.DeviceIdType.MESH
A_SLOTS = N_COL * KA
P_SLOTS = BK * PJ
WIDE = 2
CHUNKS = BC // WIDE
MB = 1024
PIECES = 4

ORDER = (
    (0, 1), (1, 0), (2, 2), (0, 3), (3, 0), (1, 1), (3, 3), (2, 0),
    (0, 2), (1, 3), (3, 1), (1, 2), (2, 1), (3, 2), (2, 3),
)
RELAY = A_SLOTS + 1

HALF, QUARTER = KA // 2, KA // 4
SIDES = (1, 3)
PIECE = ((0, 0, HALF), (1, 0, HALF), (3, 0, HALF), (2, 0, QUARTER), (2, QUARTER, QUARTER))
KEYS = (
    [("by", n) for n in SIDES]
    + [("bf", n) for n in SIDES]
    + [("a_in",), ("a_cr",), ("a_cf",)]
    + [(kind, i) for kind in ("b_in", "b_cr", "b_cf") for i in range(len(PIECE))]
    + [(kind, j, n) for kind in ("ay", "af") for j in range(4) for n in SIDES]
    + [("share", dy) for dy in range(4)]
    + [("p_own",), ("p_cr", 0), ("p_cr", 1)]
    + [("px", j, n) for j in (0, 1) for n in SIDES]
    + [("pf", n) for n in SIDES]
)
IDS = {(s,) + key: s * len(KEYS) + i for s in range(SECTIONS) for i, key in enumerate(KEYS)}
TABLE_IDS = len(IDS)
OUT_IDS = TABLE_IDS + 2
N_COPIES = OUT_IDS + CHUNKS * N_COL


def kernel(
    a_rows, a_cols, p_cols, owners, a_ref, p_ref, out_ref,
    ar0, ar1, ar2, pr0, pr1, pr2, a_dense, p_dense, acc, rounded, staged, found, tbl, ssem, rsem, lsem, tsem,
):
    a_raw, p_raw = (ar0, ar1, ar2), (pr0, pr1, pr2)
    row, col = lax.axis_index("row"), lax.axis_index("col")
    x, core = row // 2, row % 2
    y, z = col // RING, col % RING
    half = z // 2
    inside = core == half
    pair = half * 2 + (z + 1) % 2
    cross = RING - 1 - z
    cz = jnp.where(inside, z, cross)
    work_row = x * 2 + half

    def when_in(f):
        pl.when(inside)(f)

    def when_out(f):
        pl.when(jnp.logical_not(inside))(f)

    def yz(dy, dz):
        return ((y + dy) % RING) * RING + (z + dz) % RING

    def at(dy, zz):
        return ((y + dy) % RING) * RING + zz

    def xrow(dx):
        return ((x + dx) % RING) * 2 + core

    sibling = x * 2 + 1 - core

    for s in range(SECTIONS):
        a_raw[s][A_SLOTS] = jnp.zeros((TILE, TILE), jnp.bfloat16)
        p_raw[s][P_SLOTS] = jnp.zeros((TILE, TILE), jnp.bfloat16)
    rounded[BR] = jnp.zeros((WIDE, TILE, TILE), jnp.bfloat16)

    barrier = pltpu.get_barrier_semaphore()
    peers = [{"col": yz(dy, dz)} for dy, dz in ORDER]
    peers += [{"row": sibling, "col": yz(dy, dz)} for dy, dz in ((0, 0),) + ORDER]
    peers += [{"row": xrow(dx)} for dx in SIDES]
    for peer in peers:
        pl.semaphore_signal(barrier, inc=1, device_id=peer, device_id_type=MESH)
    pl.semaphore_wait(barrier, len(peers))

    def remote(src, dst, peer, i, j=None):
        return pltpu.make_async_remote_copy(
            src_ref=src, dst_ref=dst, send_sem=ssem.at[i], recv_sem=rsem.at[i if j is None else j],
            device_id=peer, device_id_type=MESH,
        )

    def a_at(s, dy, zz, lo, n):
        return a_raw[s].at[pl.ds(at(dy, zz) * KA + lo, n)]

    def b_at(s, dy, lo, n):
        start = jnp.where(inside, at(dy, z) * KA + HALF, RELAY + ((y + dy) % RING) * HALF)
        return a_raw[s].at[pl.ds(start + lo, n)]

    def origin(j):
        return (z, pair, cross, RING - 1 - pair)[j]

    def p_at(s, xx, j):
        return p_raw[s].at[pl.ds((xx * 2 + j) * 2 * PJ, 2 * PJ)]

    def msg(s, *key):
        i = IDS[(s,) + key]
        kind = key[0]
        own = a_ref.at[s, pl.ds(HALF, HALF)]
        own_a = a_ref.at[s, pl.ds(0, HALF)]
        if kind == "by":
            return remote(own, b_at(s, 0, 0, HALF), {"col": yz(key[1], 0)}, i)
        if kind == "bf":
            part = b_at(s, -key[1], 0 if key[1] == 1 else QUARTER, QUARTER)
            return remote(part, part, {"col": yz(key[1], 0)}, i)
        if kind == "a_in":
            return remote(own_a, a_at(s, 0, z, 0, HALF), {"col": at(0, pair)}, i)
        if kind == "a_cr":
            return remote(own_a, a_at(s, 0, z, 0, HALF), {"col": at(0, cross)}, i)
        if kind == "a_cf":
            part = a_at(s, 0, cross, 0, HALF)
            return remote(part, part, {"col": at(0, pair)}, i)
        if kind in ("b_in", "b_cr"):
            dy, lo, n = PIECE[key[1]]
            src = own if dy == 0 else b_at(s, dy, lo, n)
            return remote(src, a_at(s, dy, z, HALF + lo, n), {"col": at(0, pair if kind == "b_in" else cross)}, i)
        if kind == "b_cf":
            dy, lo, n = PIECE[key[1]]
            part = a_at(s, dy, cross, HALF + lo, n)
            return remote(part, part, {"col": at(0, pair)}, i)
        if kind == "ay":
            part = a_at(s, 0, origin(key[1]), 0, HALF)
            return remote(own_a if key[1] == 0 else part, part, {"col": yz(key[2], 0)}, i)
        if kind == "af":
            part = a_at(s, -key[2], origin(key[1]), 0 if key[2] == 1 else QUARTER, QUARTER)
            return remote(part, part, {"col": yz(key[2], 0)}, i)
        if kind == "share":
            part = a_raw[s].at[pl.ds(at(key[1], 0) * KA, RING * KA)]
            return remote(part, part, {"row": sibling}, i)
        if kind == "p_own":
            return remote(p_ref.at[s], p_at(s, x, core), {"row": sibling}, i)
        if kind == "p_cr":
            mine = IDS[s, "p_cr", 0] + core
            return remote(p_ref.at[s], p_at(s, x, core), {"row": work_row, "col": at(0, cross)}, mine, mine if key[1] < 0 else i)
        if kind == "px":
            part = p_at(s, x, key[1])
            return remote(part, part, {"row": xrow(key[2])}, i)
        part = p_at(s, (x - key[1]) % RING, 0 if key[1] == 1 else 1)
        return remote(part, part, {"row": xrow(key[1])}, i)

    def start(s, *key):
        msg(s, *key).start()

    def wait(s, *key):
        msg(s, *key).wait_recv()

    def kept_a(s):
        return pltpu.make_async_copy(a_ref.at[s], a_at(s, 0, z, 0, KA), lsem.at[2 * s])

    def kept_p(s):
        return pltpu.make_async_copy(p_ref.at[s], p_at(s, x, core), lsem.at[2 * s + 1])

    def own(s):
        for n in SIDES:
            start(s, "by", n)

        @when_in
        def _():
            start(s, "a_in")
            for n in SIDES:
                start(s, "ay", 0, n)
            start(s, "b_in", 0)
            kept_a(s).start()

        @when_out
        def _():
            start(s, "a_cr")
            start(s, "b_cr", 0)

    def p_own(s):
        i = IDS[s, "p_cr", 0]
        cr = remote(p_ref.at[s], p_at(s, x, core), {"row": work_row, "col": at(0, cross)}, i + core, i + core)
        cr.start()

        @when_in
        def _():
            kept_p(s).start()

        @when_out
        def _():
            start(s, "p_own")

    def p_ring(s):
        for j in (0, 1):
            for n in SIDES:
                start(s, "px", j, n)

    def p_ring_in(s):
        @when_in
        def _():
            kept_p(s).wait()
            wait(s, "p_own")
            p_ring(s)

    def p_ring_out(s):
        @when_out
        def _():
            wait(s, "p_cr", 0)
            wait(s, "p_cr", 1)
            p_ring(s)

    def p_pass(s):
        wait(s, "px", 0, 1)
        start(s, "pf", 1)
        wait(s, "px", 1, 3)
        start(s, "pf", 3)

    def p_end(s):
        wait(s, "px", 1, 1)
        wait(s, "px", 0, 3)
        for n in SIDES:
            wait(s, "pf", n)

    def ring1(s):
        for n in SIDES:
            wait(s, "by", n)
            start(s, "bf", n)

        @when_in
        def _():
            start(s, "b_in", 2)
            start(s, "b_in", 1)

        @when_out
        def _():
            start(s, "b_cr", 2)
            start(s, "b_cr", 1)

    def ring2(s):
        for i, n in ((3, 1), (4, 3)):
            wait(s, "bf", n)

            @when_in
            def _():
                start(s, "b_in", i)

            @when_out
            def _():
                start(s, "b_cr", i)

    def alpha1(s):
        @when_in
        def _():
            wait(s, "a_cr")
            start(s, "a_cf")
            for n in SIDES:
                start(s, "ay", 2, n)
            wait(s, "a_in")
            for n in SIDES:
                start(s, "ay", 1, n)

    def alpha2(s):
        @when_in
        def _():
            wait(s, "a_cf")
            for n in SIDES:
                start(s, "ay", 3, n)

    def crossed(s, pieces):
        @when_in
        def _():
            for i in pieces:
                wait(s, "b_cr", i)
                start(s, "b_cf", i)

    def alpha3(s, origins):
        @when_in
        def _():
            for j in origins:
                for n in SIDES:
                    wait(s, "ay", j, n)
                    start(s, "af", j, n)

    def share(s, dy):
        @when_in
        def _():
            for i, (at_dy, _, _) in enumerate(PIECE):
                if at_dy == dy:
                    wait(s, "b_in", i)
                    wait(s, "b_cf", i)
            if dy == 0:
                kept_a(s).wait()
            if dy == 2:
                for j in range(4):
                    for n in SIDES:
                        wait(s, "af", j, n)
            start(s, "share", dy)

    def shared(s):
        @when_out
        def _():
            for dy in range(4):
                wait(s, "share", dy)

    def find():
        def iota(shape, dim):
            return lax.broadcasted_iota(jnp.int32, shape, dim)

        def column(line):
            n = line.shape[1]
            return jnp.sum(jnp.where(iota((n, n), 0) == iota((n, n), 1), line, 0), axis=1, keepdims=True)

        spots = iota((N_COL, BR * BK), 1)
        first = iota((N_COL, BR * BK), 0) * KA
        for s in range(SECTIONS):
            codes = a_rows[s] * BK + a_cols[s]
            best = jnp.full((N_COL, BR * BK), A_SLOTS, jnp.int32)
            for t in range(KA):
                best = jnp.minimum(best, jnp.where(column(codes[t : t + 1]) == spots, first + t, A_SLOTS))
            found[0, s : s + 1, :] = jnp.min(best, axis=0, keepdims=True)
        n_row = BK // 2
        spots = iota((n_row, BK * BC), 1)
        group = iota((n_row, BK * BC), 0)
        for s in range(SECTIONS):
            best = jnp.full((n_row, BK * BC), P_SLOTS, jnp.int32)
            for m in range(2):
                cols = p_cols[s, m]
                k = group * 2 + m
                for j in range(PJ):
                    best = jnp.minimum(best, jnp.where(k * BC + column(cols[j : j + 1]) == spots, k * PJ + j, P_SLOTS))
            found[1, s : s + 1, : BK * BC] = jnp.min(best, axis=0, keepdims=True)
        line = iota((BR, TILE), 0)
        spots = iota((BR, TILE), 1)
        named = column(owners[...]) == spots // MOST
        low = jnp.min(jnp.where(named, line, BR), axis=0, keepdims=True)
        high = jnp.max(jnp.where(named, line, -1), axis=0, keepdims=True)
        second = jnp.where(high > low, high, BR)
        slot = iota((1, TILE), 1) % MOST
        found[0, SECTIONS : SECTIONS + 1, :TILE] = jnp.where(slot == 0, low, second)

    def table_msgs():
        return (
            remote(found.at[0], found.at[0], {"row": sibling}, TABLE_IDS),
            remote(found.at[1], found.at[1], {"col": at(0, cross)}, TABLE_IDS + 1),
        )

    def find_tables():
        @when_in
        def _():
            find()
            for copy in table_msgs():
                copy.start()

    def take_tables():
        @when_out
        def _():
            for copy in table_msgs():
                copy.wait_recv()

        copy = pltpu.make_async_copy(found, tbl, tsem)
        copy.start()
        copy.wait()

    def place_p(s):
        @pl.loop(0, BK)
        def _(k):
            for c in range(BC):
                p_dense[pl.ds(pl.multiple_of(k * TILE, TILE), TILE), c * TILE : (c + 1) * TILE] = p_raw[s][
                    tbl[1, s, k * BC + c]
                ]

    def place_a(s):
        @pl.loop(0, BR)
        def _(r):
            for k in range(BK):
                a_dense[pl.ds(pl.multiple_of(r * TILE, TILE), TILE), k * TILE : (k + 1) * TILE] = a_raw[s][
                    tbl[0, s, r * BK + k]
                ]

    def part_dot(mb, nb):
        rows = pl.ds(pl.multiple_of(mb * MB, MB), MB)
        return jnp.dot(
            a_dense[rows, :], p_dense[:, nb * WIDE * TILE : (nb + 1) * WIDE * TILE], preferred_element_type=jnp.float32
        )

    def dots(s, nb):
        @pl.loop(0, BR * TILE // MB)
        def _(mb):
            rows = pl.ds(pl.multiple_of(mb * MB, MB), MB)
            value = part_dot(mb, nb)
            if s == 0:
                acc[nb, rows, :] = value
            else:
                acc[nb, rows, :] += value

    def finish(nb):
        @pl.loop(0, BR * TILE // MB)
        def _(mb):
            rows = pl.ds(pl.multiple_of(mb * MB, MB), MB)
            value = (acc[nb, rows, :] + part_dot(mb, nb)).astype(jnp.bfloat16)
            for i in range(MB // TILE):
                for j in range(WIDE):
                    rounded[mb * (MB // TILE) + i, j] = value[i * TILE : (i + 1) * TILE, j * TILE : (j + 1) * TILE]

        @pl.loop(0, N_COL)
        def _(o):
            for q in range(MOST):
                staged[nb, o, q] = rounded[tbl[0, SECTIONS, o * MOST + q]]

        @when_in
        def _():
            out_own(nb).start()

        @when_out
        def _():
            out_msg(nb, 0, 0).start()

        for dy, dz in ORDER:
            out_msg(nb, dy, dz).start()

    def out_at(nb, c):
        return out_ref.at[:, pl.ds(c * BC + nb * WIDE, WIDE)]

    def out_own(nb):
        return pltpu.make_async_copy(staged.at[nb, col], out_at(nb, col), lsem.at[2 * SECTIONS + nb])

    def out_msg(nb, dy, dz):
        base = OUT_IDS + nb * N_COL
        c = at(0, cz)
        o = yz(dy, dz)
        return remote(staged.at[nb, o], out_at(nb, c), {"row": work_row, "col": o}, base + o, base + c)

    def out_wait(nb):
        @pl.loop(0, N_COL)
        def _(c):
            @pl.when(jnp.logical_not(inside & (c == col)))
            def _():
                i = OUT_IDS + nb * N_COL + c
                remote(staged.at[nb, c], out_at(nb, c), {"row": sibling}, i, i).wait_recv()

    def sent():
        for s in range(SECTIONS):
            i = IDS[s, "p_cr", 0] + core
            remote(p_ref.at[s], p_at(s, x, core), {"row": work_row, "col": at(0, cross)}, i, i).wait_send()
            for key in KEYS:
                if key[0] in ("by", "bf", "px", "pf"):
                    msg(s, *key).wait_send()

        @when_in
        def _():
            for s in range(SECTIONS):
                for key in KEYS:
                    if key[0] in ("a_in", "a_cf", "b_in", "b_cf", "ay", "af", "share"):
                        msg(s, *key).wait_send()
            for copy in table_msgs():
                copy.wait_send()

        @when_out
        def _():
            for s in range(SECTIONS):
                for key in KEYS:
                    if key[0] in ("a_cr", "b_cr", "p_own"):
                        msg(s, *key).wait_send()

    def out_sent(nb):
        @when_in
        def _():
            out_own(nb).wait()

        @when_out
        def _():
            out_msg(nb, 0, 0).wait_send()

        for dy, dz in ORDER:
            out_msg(nb, dy, dz).wait_send()

    def moves(s):
        return [
            lambda: ring1(s),
            lambda: alpha1(s),
            lambda: p_ring_out(s),
            lambda: ring2(s),
            lambda: alpha2(s),
            lambda: crossed(s, (0, 1, 2)),
            lambda: p_pass(s),
            lambda: alpha3(s, (0,)),
            lambda: crossed(s, (3, 4)),
            lambda: alpha3(s, (2, 1)),
            lambda: share(s, 0),
            lambda: alpha3(s, (3,)),
            lambda: share(s, 1),
            lambda: share(s, 3),
            lambda: share(s, 2),
        ]

    def work(s):
        def first():
            p_end(s)
            place_p(s)
            shared(s)
            place_a(s)

        return [first] + [lambda nb=nb: dots(s, nb) for nb in range(1)]

    def mix(many, few):
        done = 0
        for i, f in enumerate(many):
            f()
            while done * len(many) < (i + 1) * len(few):
                few[done]()
                done += 1

    for step in plan(own, p_own, p_ring_in, find_tables, take_tables, moves, work):
        step()
    work(2)[0]()
    finish(0)
    for chunks in (range(1, 2), range(2, CHUNKS)):
        for s in range(SECTIONS):
            place_p(s)
            place_a(s)
            for nb in chunks:
                if s < SECTIONS - 1:
                    dots(s, nb)
                else:
                    finish(nb)
    sent()
    for nb in range(CHUNKS):
        out_sent(nb)
        out_wait(nb)


EARLY = 2
LAG = 3
TABLES = 8
AFTER = 15


def plan(own, p_own, p_ring_in, find_tables, take_tables, moves, work):
    steps = []
    for s in range(SECTIONS):
        if s < EARLY:
            steps += [functools.partial(own, s), functools.partial(p_own, s)]
        if s == 0:
            steps += [functools.partial(p_ring_in, 0)]
    timed = []
    for s in range(SECTIONS):
        for i, f in enumerate(moves(s)):
            timed.append((s * LAG + i, s, f))
        if s >= EARLY:
            timed.append((s * LAG - 3, s, functools.partial(own, s)))
            timed.append((s * LAG - 3, s, functools.partial(p_own, s)))
        if s:
            timed.append((s * LAG / 2 + 1 if s < EARLY else s * LAG - 2, s, functools.partial(p_ring_in, s)))
    timed.append((TABLES, 0, find_tables))
    timed.append((AFTER, 0, take_tables))
    for s in range(SECTIONS - 1):
        for i, f in enumerate(work(s)):
            timed.append((s * LAG + AFTER + i, 9, f))
    timed.sort(key=lambda t: t[:2])
    return steps + [f for _, _, f in timed]


def settle(held, out_ref, sems):
    n = N_COL * BC // PIECES
    copies = []
    for q in range(MOST):
        for i in range(PIECES):
            part = (q, pl.ds(i * n, n))
            copies.append(pltpu.make_async_copy(held.at[part], out_ref.at[part], sems.at[q * PIECES + i]))
            copies[-1].start()
    for copy in copies:
        copy.wait()


def body(a_tiles, a_rows, a_cols, p_tiles, p_cols, owners):
    a = a_tiles.reshape(SECTIONS, KA, TILE, TILE)
    p = p_tiles.reshape(SECTIONS, 2 * PJ, TILE, TILE)
    bf = jnp.bfloat16
    vmem = pl.BlockSpec(memory_space=pltpu.VMEM)
    hbm = pl.BlockSpec(memory_space=pl.ANY)
    shape = (MOST, N_COL * BC, TILE, TILE)
    held = pl.pallas_call(
        kernel,
        name="block_product",
        out_shape=pltpu.VMEM(shape, bf),
        in_specs=[vmem] * 4 + [hbm] * 2,
        out_specs=vmem,
        scratch_shapes=[pltpu.VMEM((RELAY + RING * HALF, TILE, TILE), bf)] * SECTIONS
        + [pltpu.VMEM((P_SLOTS + 1, TILE, TILE), bf)] * SECTIONS
        + [
            pltpu.VMEM((BR * TILE, BK * TILE), bf),
            pltpu.VMEM((BK * TILE, BC * TILE), bf),
            pltpu.VMEM((CHUNKS, BR * TILE, WIDE * TILE), jnp.float32),
            pltpu.VMEM((BR + 1, WIDE, TILE, TILE), bf),
            pltpu.VMEM((CHUNKS, N_COL, MOST, WIDE, TILE, TILE), bf),
            pltpu.VMEM((2, 8, BR * BK), jnp.int32),
            pltpu.SMEM((2, 8, BR * BK), jnp.int32),
            pltpu.SemaphoreType.DMA((N_COPIES,)),
            pltpu.SemaphoreType.DMA((N_COPIES,)),
            pltpu.SemaphoreType.DMA((2 * SECTIONS + CHUNKS,)),
            pltpu.SemaphoreType.DMA,
        ],
        compiler_params=pltpu.CompilerParams(collective_id=0, has_side_effects=True, vmem_limit_bytes=52 << 20),
        cost_estimate=pl.CostEstimate(flops=25_769_803_776, bytes_accessed=20_000_000, transcendentals=0),
    )(
        jnp.transpose(a_rows[0], (1, 2, 0)),
        jnp.transpose(a_cols[0], (1, 2, 0)),
        jnp.transpose(p_cols[:, :, :, 0], (1, 2, 3, 0)),
        owners.reshape(1, BR),
        a,
        p,
    )
    return pl.pallas_call(
        settle,
        name="settle",
        out_shape=jax.ShapeDtypeStruct(shape, bf),
        in_specs=[vmem],
        out_specs=hbm,
        scratch_shapes=[pltpu.SemaphoreType.DMA((MOST * PIECES,))],
        compiler_params=pltpu.CompilerParams(vmem_limit_bytes=2 << 20),
    )(held)


def solution(mesh):
    placed = (
        P("row", "col", None, None, None, None),
        P("row", None, None, None),
        P("row", None, None, None),
        P("row", None, None, "col", None, None, None),
        P(None, None, None, "col", None),
        P("row", None),
    )
    return jax.shard_map(
        body,
        mesh=mesh,
        in_specs=placed,
        out_specs=P(("row", "col"), None, None, None),
        check_vma=False,
    )
```

```python
import functools

import jax
import jax.numpy as jnp
from jax import lax
from jax.experimental import pallas as pl
from jax.experimental.pallas import tpu as pltpu
from jax.sharding import PartitionSpec as P

SECTIONS = 3
BR = 16
BK = 16
BC = 8
KA = 8
PJ = 4
MOST = 2
TILE = 128
N_COL = 16
RING = 4
MESH = pl.DeviceIdType.MESH
A_SLOTS = N_COL * KA
P_SLOTS = BK * PJ
WIDE = 2
CHUNKS = BC // WIDE
MB = 1024
PIECES = 4

ORDER = (
    (0, 1), (1, 0), (2, 2), (0, 3), (3, 0), (1, 1), (3, 3), (2, 0),
    (0, 2), (1, 3), (3, 1), (1, 2), (2, 1), (3, 2), (2, 3),
)
RELAY = A_SLOTS + 1

HALF, QUARTER = KA // 2, KA // 4
SIDES = (1, 3)
PIECE = ((0, 0, HALF), (1, 0, HALF), (3, 0, HALF), (2, 0, QUARTER), (2, QUARTER, QUARTER))
KEYS = (
    [("by", n) for n in SIDES]
    + [("bf", n) for n in SIDES]
    + [("a_in",), ("a_cr",), ("a_cf",)]
    + [(kind, i) for kind in ("b_in", "b_cr", "b_cf") for i in range(len(PIECE))]
    + [(kind, j, n) for kind in ("ay", "af") for j in range(4) for n in SIDES]
    + [("share", dy) for dy in range(4)]
    + [("p_own",), ("p_cr", 0), ("p_cr", 1)]
    + [("px", j, n) for j in (0, 1) for n in SIDES]
    + [("pf", n) for n in SIDES]
)
IDS = {(s,) + key: s * len(KEYS) + i for s in range(SECTIONS) for i, key in enumerate(KEYS)}
TABLE_IDS = len(IDS)
OUT_IDS = TABLE_IDS + 2
TURN = 4
N_COPIES = OUT_IDS + CHUNKS * N_COL


def kernel(
    a_rows, a_cols, p_cols, owners, a_ref, p_ref, out_ref,
    ar0, ar1, ar2, pr0, pr1, pr2, a_dense, p_dense, acc, rounded, staged, found, tbl, ssem, rsem, lsem, tsem,
):
    a_raw, p_raw = (ar0, ar1, ar2), (pr0, pr1, pr2)
    row, col = lax.axis_index("row"), lax.axis_index("col")
    x, core = row // 2, row % 2
    y, z = col // RING, col % RING
    half = z // 2
    inside = core == half
    pair = half * 2 + (z + 1) % 2
    cross = RING - 1 - z
    cz = jnp.where(inside, z, cross)
    work_row = x * 2 + half

    def when_in(f):
        pl.when(inside)(f)

    def when_out(f):
        pl.when(jnp.logical_not(inside))(f)

    def yz(dy, dz):
        return ((y + dy) % RING) * RING + (z + dz) % RING

    def at(dy, zz):
        return ((y + dy) % RING) * RING + zz

    def xrow(dx):
        return ((x + dx) % RING) * 2 + core

    sibling = x * 2 + 1 - core

    for s in range(SECTIONS):
        a_raw[s][A_SLOTS] = jnp.zeros((TILE, TILE), jnp.bfloat16)
        p_raw[s][P_SLOTS] = jnp.zeros((TILE, TILE), jnp.bfloat16)
    rounded[BR] = jnp.zeros((WIDE, TILE, TILE), jnp.bfloat16)

    barrier = pltpu.get_barrier_semaphore()
    peers = [{"col": yz(dy, dz)} for dy, dz in ORDER]
    peers += [{"row": sibling, "col": yz(dy, dz)} for dy, dz in ((0, 0),) + ORDER]
    peers += [{"row": xrow(dx)} for dx in SIDES]
    for peer in peers:
        pl.semaphore_signal(barrier, inc=1, device_id=peer, device_id_type=MESH)
    pl.semaphore_wait(barrier, len(peers))

    def remote(src, dst, peer, i, j=None):
        return pltpu.make_async_remote_copy(
            src_ref=src, dst_ref=dst, send_sem=ssem.at[i], recv_sem=rsem.at[i if j is None else j],
            device_id=peer, device_id_type=MESH,
        )

    def a_at(s, dy, zz, lo, n):
        return a_raw[s].at[pl.ds(at(dy, zz) * KA + lo, n)]

    def b_at(s, dy, lo, n):
        start = jnp.where(inside, at(dy, z) * KA + HALF, RELAY + ((y + dy) % RING) * HALF)
        return a_raw[s].at[pl.ds(start + lo, n)]

    def origin(j):
        return (z, pair, cross, RING - 1 - pair)[j]

    def p_at(s, xx, j):
        return p_raw[s].at[pl.ds((xx * 2 + j) * 2 * PJ, 2 * PJ)]

    def msg(s, *key):
        i = IDS[(s,) + key]
        kind = key[0]
        own = a_ref.at[s, pl.ds(HALF, HALF)]
        own_a = a_ref.at[s, pl.ds(0, HALF)]
        if kind == "by":
            return remote(own, b_at(s, 0, 0, HALF), {"col": yz(key[1], 0)}, i)
        if kind == "bf":
            part = b_at(s, -key[1], 0 if key[1] == 1 else QUARTER, QUARTER)
            return remote(part, part, {"col": yz(key[1], 0)}, i)
        if kind == "a_in":
            return remote(own_a, a_at(s, 0, z, 0, HALF), {"col": at(0, pair)}, i)
        if kind == "a_cr":
            return remote(own_a, a_at(s, 0, z, 0, HALF), {"col": at(0, cross)}, i)
        if kind == "a_cf":
            part = a_at(s, 0, cross, 0, HALF)
            return remote(part, part, {"col": at(0, pair)}, i)
        if kind in ("b_in", "b_cr"):
            dy, lo, n = PIECE[key[1]]
            src = own if dy == 0 else b_at(s, dy, lo, n)
            return remote(src, a_at(s, dy, z, HALF + lo, n), {"col": at(0, pair if kind == "b_in" else cross)}, i)
        if kind == "b_cf":
            dy, lo, n = PIECE[key[1]]
            part = a_at(s, dy, cross, HALF + lo, n)
            return remote(part, part, {"col": at(0, pair)}, i)
        if kind == "ay":
            part = a_at(s, 0, origin(key[1]), 0, HALF)
            return remote(own_a if key[1] == 0 else part, part, {"col": yz(key[2], 0)}, i)
        if kind == "af":
            part = a_at(s, -key[2], origin(key[1]), 0 if key[2] == 1 else QUARTER, QUARTER)
            return remote(part, part, {"col": yz(key[2], 0)}, i)
        if kind == "share":
            part = a_raw[s].at[pl.ds(at(key[1], 0) * KA, RING * KA)]
            return remote(part, part, {"row": sibling}, i)
        if kind == "p_own":
            return remote(p_ref.at[s], p_at(s, x, core), {"row": sibling}, i)
        if kind == "p_cr":
            mine = IDS[s, "p_cr", 0] + core
            return remote(p_ref.at[s], p_at(s, x, core), {"row": work_row, "col": at(0, cross)}, mine, mine if key[1] < 0 else i)
        if kind == "px":
            part = p_at(s, x, key[1])
            return remote(part, part, {"row": xrow(key[2])}, i)
        part = p_at(s, (x - key[1]) % RING, 0 if key[1] == 1 else 1)
        return remote(part, part, {"row": xrow(key[1])}, i)

    def start(s, *key):
        msg(s, *key).start()

    def wait(s, *key):
        msg(s, *key).wait_recv()

    def kept_a(s):
        return pltpu.make_async_copy(a_ref.at[s], a_at(s, 0, z, 0, KA), lsem.at[2 * s])

    def kept_p(s):
        return pltpu.make_async_copy(p_ref.at[s], p_at(s, x, core), lsem.at[2 * s + 1])

    def own(s):
        for n in SIDES:
            start(s, "by", n)

        @when_in
        def _():
            start(s, "a_in")
            for n in SIDES:
                start(s, "ay", 0, n)
            start(s, "b_in", 0)
            kept_a(s).start()

        @when_out
        def _():
            start(s, "a_cr")
            start(s, "b_cr", 0)

    def p_own(s):
        i = IDS[s, "p_cr", 0]
        cr = remote(p_ref.at[s], p_at(s, x, core), {"row": work_row, "col": at(0, cross)}, i + core, i + core)
        cr.start()

        @when_in
        def _():
            kept_p(s).start()

        @when_out
        def _():
            start(s, "p_own")

    def p_ring(s):
        for j in (0, 1):
            for n in SIDES:
                start(s, "px", j, n)

    def p_ring_in(s):
        @when_in
        def _():
            kept_p(s).wait()
            wait(s, "p_own")
            p_ring(s)

    def p_ring_out(s):
        @when_out
        def _():
            wait(s, "p_cr", 0)
            wait(s, "p_cr", 1)
            p_ring(s)

    def p_pass(s):
        wait(s, "px", 0, 1)
        start(s, "pf", 1)
        wait(s, "px", 1, 3)
        start(s, "pf", 3)

    def p_end(s):
        wait(s, "px", 1, 1)
        wait(s, "px", 0, 3)
        for n in SIDES:
            wait(s, "pf", n)

    def ring1(s):
        for n in SIDES:
            wait(s, "by", n)
            start(s, "bf", n)

        @when_in
        def _():
            start(s, "b_in", 2)
            start(s, "b_in", 1)

        @when_out
        def _():
            start(s, "b_cr", 2)
            start(s, "b_cr", 1)

    def ring2(s):
        for i, n in ((3, 1), (4, 3)):
            wait(s, "bf", n)

            @when_in
            def _():
                start(s, "b_in", i)

            @when_out
            def _():
                start(s, "b_cr", i)

    def alpha1(s):
        @when_in
        def _():
            wait(s, "a_cr")
            start(s, "a_cf")
            for n in SIDES:
                start(s, "ay", 2, n)
            wait(s, "a_in")
            for n in SIDES:
                start(s, "ay", 1, n)

    def alpha2(s):
        @when_in
        def _():
            wait(s, "a_cf")
            for n in SIDES:
                start(s, "ay", 3, n)

    def crossed(s, pieces):
        @when_in
        def _():
            for i in pieces:
                wait(s, "b_cr", i)
                start(s, "b_cf", i)

    def alpha3(s, origins):
        @when_in
        def _():
            for j in origins:
                for n in SIDES:
                    wait(s, "ay", j, n)
                    start(s, "af", j, n)

    def share(s, dy):
        @when_in
        def _():
            for i, (at_dy, _, _) in enumerate(PIECE):
                if at_dy == dy:
                    wait(s, "b_in", i)
                    wait(s, "b_cf", i)
            if dy == 0:
                kept_a(s).wait()
            if dy == 2:
                for j in range(4):
                    for n in SIDES:
                        wait(s, "af", j, n)
            start(s, "share", dy)

    def shared(s):
        @when_out
        def _():
            for dy in range(4):
                wait(s, "share", dy)

    def find():
        def iota(shape, dim):
            return lax.broadcasted_iota(jnp.int32, shape, dim)

        def column(line):
            n = line.shape[1]
            return jnp.sum(jnp.where(iota((n, n), 0) == iota((n, n), 1), line, 0), axis=1, keepdims=True)

        spots = iota((N_COL, BR * BK), 1)
        first = iota((N_COL, BR * BK), 0) * KA
        for s in range(SECTIONS):
            codes = a_rows[s] * BK + a_cols[s]
            best = jnp.full((N_COL, BR * BK), A_SLOTS, jnp.int32)
            for t in range(KA):
                best = jnp.minimum(best, jnp.where(column(codes[t : t + 1]) == spots, first + t, A_SLOTS))
            found[0, s : s + 1, :] = jnp.min(best, axis=0, keepdims=True)
        n_row = BK // 2
        spots = iota((n_row, BK * BC), 1)
        group = iota((n_row, BK * BC), 0)
        for s in range(SECTIONS):
            best = jnp.full((n_row, BK * BC), P_SLOTS, jnp.int32)
            for m in range(2):
                cols = p_cols[s, m]
                k = group * 2 + m
                for j in range(PJ):
                    best = jnp.minimum(best, jnp.where(k * BC + column(cols[j : j + 1]) == spots, k * PJ + j, P_SLOTS))
            found[1, s : s + 1, : BK * BC] = jnp.min(best, axis=0, keepdims=True)
        line = iota((BR, TILE), 0)
        spots = iota((BR, TILE), 1)
        named = column(owners[...]) == spots // MOST
        low = jnp.min(jnp.where(named, line, BR), axis=0, keepdims=True)
        high = jnp.max(jnp.where(named, line, -1), axis=0, keepdims=True)
        second = jnp.where(high > low, high, BR)
        slot = iota((1, TILE), 1) % MOST
        found[0, SECTIONS : SECTIONS + 1, :TILE] = jnp.where(slot == 0, low, second)

    def table_msgs():
        return (
            remote(found.at[0], found.at[0], {"row": sibling}, TABLE_IDS),
            remote(found.at[1], found.at[1], {"col": at(0, cross)}, TABLE_IDS + 1),
        )

    def find_tables():
        @when_in
        def _():
            find()
            for copy in table_msgs():
                copy.start()

    def take_tables():
        @when_out
        def _():
            for copy in table_msgs():
                copy.wait_recv()

        copy = pltpu.make_async_copy(found, tbl, tsem)
        copy.start()
        copy.wait()

    def place_p(s):
        @pl.loop(0, BK)
        def _(k):
            for c in range(BC):
                p_dense[pl.ds(pl.multiple_of(k * TILE, TILE), TILE), c * TILE : (c + 1) * TILE] = p_raw[s][
                    tbl[1, s, k * BC + c]
                ]

    def place_a(s):
        @pl.loop(0, BR)
        def _(r):
            for k in range(BK):
                a_dense[pl.ds(pl.multiple_of(r * TILE, TILE), TILE), k * TILE : (k + 1) * TILE] = a_raw[s][
                    tbl[0, s, r * BK + k]
                ]

    def part_dot(mb, nb):
        rows = pl.ds(pl.multiple_of(mb * MB, MB), MB)
        return jnp.dot(
            a_dense[rows, :], p_dense[:, nb * WIDE * TILE : (nb + 1) * WIDE * TILE], preferred_element_type=jnp.float32
        )

    def dots(s, nb):
        @pl.loop(0, BR * TILE // MB)
        def _(mb):
            rows = pl.ds(pl.multiple_of(mb * MB, MB), MB)
            value = part_dot(mb, nb)
            if s == 0:
                acc[nb, rows, :] = value
            else:
                acc[nb, rows, :] += value

    def finish(nb):
        @pl.loop(0, BR * TILE // MB)
        def _(mb):
            rows = pl.ds(pl.multiple_of(mb * MB, MB), MB)
            value = (acc[nb, rows, :] + part_dot(mb, nb)).astype(jnp.bfloat16)
            for i in range(MB // TILE):
                for j in range(WIDE):
                    rounded[mb * (MB // TILE) + i, j] = value[i * TILE : (i + 1) * TILE, j * TILE : (j + 1) * TILE]

        @pl.loop(0, N_COL)
        def _(o):
            for q in range(MOST):
                staged[nb, o, q] = rounded[tbl[0, SECTIONS, o * MOST + q]]

        @when_in
        def _():
            out_own(nb).start()

        @when_out
        def _():
            out_msg(nb, 0, 0).start()

        for dy, dz in out_order():
            out_msg(nb, dy, dz).start()

    def out_at(nb, c):
        return out_ref.at[:, pl.ds(c * BC + nb * WIDE, WIDE)]

    def out_own(nb):
        return pltpu.make_async_copy(staged.at[nb, col], out_at(nb, col), lsem.at[2 * SECTIONS + nb])

    def out_msg(nb, dy, dz):
        base = OUT_IDS + nb * N_COL
        c = at(0, cz)
        o = yz(dy, dz)
        return remote(staged.at[nb, o], out_at(nb, c), {"row": work_row, "col": o}, base + o, base + c)

    def out_wait(nb):
        @pl.loop(0, N_COL)
        def _(c):
            @pl.when(jnp.logical_not(inside & (c == col)))
            def _():
                i = OUT_IDS + nb * N_COL + c
                remote(staged.at[nb, c], out_at(nb, c), {"row": sibling}, i, i).wait_recv()

    def sent():
        for s in range(SECTIONS):
            i = IDS[s, "p_cr", 0] + core
            remote(p_ref.at[s], p_at(s, x, core), {"row": work_row, "col": at(0, cross)}, i, i).wait_send()
            for key in KEYS:
                if key[0] in ("by", "bf", "px", "pf"):
                    msg(s, *key).wait_send()

        @when_in
        def _():
            for s in range(SECTIONS):
                for key in KEYS:
                    if key[0] in ("a_in", "a_cf", "b_in", "b_cf", "ay", "af", "share"):
                        msg(s, *key).wait_send()
            for copy in table_msgs():
                copy.wait_send()

        @when_out
        def _():
            for s in range(SECTIONS):
                for key in KEYS:
                    if key[0] in ("a_cr", "b_cr", "p_own"):
                        msg(s, *key).wait_send()

    def out_order():
        for (dy, dz), (oy, oz) in zip(ORDER, ORDER[TURN:] + ORDER[:TURN]):
            yield jnp.where(inside, dy, oy), jnp.where(inside, dz, oz)

    def out_sent(nb):
        @when_in
        def _():
            out_own(nb).wait()

        @when_out
        def _():
            out_msg(nb, 0, 0).wait_send()

        for dy, dz in ORDER:
            out_msg(nb, dy, dz).wait_send()

    def moves(s):
        return [
            lambda: ring1(s),
            lambda: alpha1(s),
            lambda: p_ring_out(s),
            lambda: ring2(s),
            lambda: alpha2(s),
            lambda: crossed(s, (0, 1, 2)),
            lambda: p_pass(s),
            lambda: alpha3(s, (0,)),
            lambda: crossed(s, (3, 4)),
            lambda: alpha3(s, (2, 1)),
            lambda: share(s, 0),
            lambda: alpha3(s, (3,)),
            lambda: share(s, 1),
            lambda: share(s, 3),
            lambda: share(s, 2),
        ]

    def work(s):
        def first():
            p_end(s)
            place_p(s)
            shared(s)
            place_a(s)

        return [first] + [lambda nb=nb: dots(s, nb) for nb in range(1)]

    def mix(many, few):
        done = 0
        for i, f in enumerate(many):
            f()
            while done * len(many) < (i + 1) * len(few):
                few[done]()
                done += 1

    for step in plan(own, p_own, p_ring_in, find_tables, take_tables, moves, work):
        step()
    work(2)[0]()
    finish(0)
    for chunks in (range(1, 2), range(2, CHUNKS)):
        for s in range(SECTIONS):
            place_p(s)
            place_a(s)
            for nb in chunks:
                if s < SECTIONS - 1:
                    dots(s, nb)
                else:
                    finish(nb)
    sent()
    for nb in range(CHUNKS):
        out_sent(nb)
        out_wait(nb)


EARLY = 2
LAG = 3
TABLES = 8
AFTER = 15


def plan(own, p_own, p_ring_in, find_tables, take_tables, moves, work):
    steps = []
    for s in range(SECTIONS):
        if s < EARLY:
            steps += [functools.partial(own, s), functools.partial(p_own, s)]
        if s == 0:
            steps += [functools.partial(p_ring_in, 0)]
    timed = []
    for s in range(SECTIONS):
        for i, f in enumerate(moves(s)):
            timed.append((s * LAG + i, s, f))
        if s >= EARLY:
            timed.append((s * LAG - 3, s, functools.partial(own, s)))
            timed.append((s * LAG - 3, s, functools.partial(p_own, s)))
        if s:
            timed.append((s * LAG / 2 + 1 if s < EARLY else s * LAG - 2, s, functools.partial(p_ring_in, s)))
    timed.append((TABLES, 0, find_tables))
    timed.append((AFTER, 0, take_tables))
    for s in range(SECTIONS - 1):
        for i, f in enumerate(work(s)):
            timed.append((s * LAG + AFTER + i, 9, f))
    timed.sort(key=lambda t: t[:2])
    return steps + [f for _, _, f in timed]


def settle(held, out_ref, sems):
    n = N_COL * BC // PIECES
    copies = []
    for q in range(MOST):
        for i in range(PIECES):
            part = (q, pl.ds(i * n, n))
            copies.append(pltpu.make_async_copy(held.at[part], out_ref.at[part], sems.at[q * PIECES + i]))
            copies[-1].start()
    for copy in copies:
        copy.wait()


def body(a_tiles, a_rows, a_cols, p_tiles, p_cols, owners):
    a = a_tiles.reshape(SECTIONS, KA, TILE, TILE)
    p = p_tiles.reshape(SECTIONS, 2 * PJ, TILE, TILE)
    bf = jnp.bfloat16
    vmem = pl.BlockSpec(memory_space=pltpu.VMEM)
    hbm = pl.BlockSpec(memory_space=pl.ANY)
    shape = (MOST, N_COL * BC, TILE, TILE)
    held = pl.pallas_call(
        kernel,
        name="block_product",
        out_shape=pltpu.VMEM(shape, bf),
        in_specs=[vmem] * 4 + [hbm] * 2,
        out_specs=vmem,
        scratch_shapes=[pltpu.VMEM((RELAY + RING * HALF, TILE, TILE), bf)] * SECTIONS
        + [pltpu.VMEM((P_SLOTS + 1, TILE, TILE), bf)] * SECTIONS
        + [
            pltpu.VMEM((BR * TILE, BK * TILE), bf),
            pltpu.VMEM((BK * TILE, BC * TILE), bf),
            pltpu.VMEM((CHUNKS, BR * TILE, WIDE * TILE), jnp.float32),
            pltpu.VMEM((BR + 1, WIDE, TILE, TILE), bf),
            pltpu.VMEM((CHUNKS, N_COL, MOST, WIDE, TILE, TILE), bf),
            pltpu.VMEM((2, 8, BR * BK), jnp.int32),
            pltpu.SMEM((2, 8, BR * BK), jnp.int32),
            pltpu.SemaphoreType.DMA((N_COPIES,)),
            pltpu.SemaphoreType.DMA((N_COPIES,)),
            pltpu.SemaphoreType.DMA((2 * SECTIONS + CHUNKS,)),
            pltpu.SemaphoreType.DMA,
        ],
        compiler_params=pltpu.CompilerParams(collective_id=0, has_side_effects=True, vmem_limit_bytes=52 << 20),
        cost_estimate=pl.CostEstimate(flops=25_769_803_776, bytes_accessed=20_000_000, transcendentals=0),
    )(
        jnp.transpose(a_rows[0], (1, 2, 0)),
        jnp.transpose(a_cols[0], (1, 2, 0)),
        jnp.transpose(p_cols[:, :, :, 0], (1, 2, 3, 0)),
        owners.reshape(1, BR),
        a,
        p,
    )
    return pl.pallas_call(
        settle,
        name="settle",
        out_shape=jax.ShapeDtypeStruct(shape, bf),
        in_specs=[vmem],
        out_specs=hbm,
        scratch_shapes=[pltpu.SemaphoreType.DMA((MOST * PIECES,))],
        compiler_params=pltpu.CompilerParams(vmem_limit_bytes=2 << 20),
    )(held)


def solution(mesh):
    placed = (
        P("row", "col", None, None, None, None),
        P("row", None, None, None),
        P("row", None, None, None),
        P("row", None, None, "col", None, None, None),
        P(None, None, None, "col", None),
        P("row", None),
    )
    return jax.shard_map(
        body,
        mesh=mesh,
        in_specs=placed,
        out_specs=P(("row", "col"), None, None, None),
        check_vma=False,
    )
```

```python
import functools

import jax
import jax.numpy as jnp
from jax import lax
from jax.experimental import pallas as pl
from jax.experimental.pallas import tpu as pltpu
from jax.sharding import PartitionSpec as P

SECTIONS = 3
BR = 16
BK = 16
BC = 8
KA = 8
PJ = 4
MOST = 2
TILE = 128
N_COL = 16
RING = 4
MESH = pl.DeviceIdType.MESH
A_SLOTS = N_COL * KA
P_SLOTS = BK * PJ
WIDE = 2
CHUNKS = BC // WIDE
MB = 1024
PIECES = 4

ORDER = (
    (0, 1), (1, 0), (2, 2), (0, 3), (3, 0), (1, 1), (3, 3), (2, 0),
    (0, 2), (1, 3), (3, 1), (1, 2), (2, 1), (3, 2), (2, 3),
)
RELAY = A_SLOTS + 1

HALF, QUARTER = KA // 2, KA // 4
SIDES = (1, 3)
PIECE = ((0, 0, HALF), (1, 0, HALF), (3, 0, HALF), (2, 0, QUARTER), (2, QUARTER, QUARTER))
KEYS = (
    [("by", n) for n in SIDES]
    + [("bf", n) for n in SIDES]
    + [("a_in",), ("a_cr",), ("a_cf",)]
    + [(kind, i) for kind in ("b_in", "b_cr", "b_cf") for i in range(len(PIECE))]
    + [(kind, j, n) for kind in ("ay", "af") for j in range(4) for n in SIDES]
    + [("share", dy) for dy in range(4)]
    + [("p_own",), ("p_cr", 0), ("p_cr", 1)]
    + [("px", j, n) for j in (0, 1) for n in SIDES]
    + [("pf", n) for n in SIDES]
)
IDS = {(s,) + key: s * len(KEYS) + i for s in range(SECTIONS) for i, key in enumerate(KEYS)}
TABLE_IDS = len(IDS)
OUT_IDS = TABLE_IDS + 3
TURN = 4
N_COPIES = OUT_IDS + CHUNKS * N_COL


def kernel(
    a_rows, a_cols, p_cols, owners, a_ref, p_ref, out_ref,
    ar0, ar1, ar2, pr0, pr1, pr2, a_dense, p_dense, acc, rounded, staged, found, taken, tbl, ssem, rsem, lsem, tsem,
):
    a_raw, p_raw = (ar0, ar1, ar2), (pr0, pr1, pr2)
    row, col = lax.axis_index("row"), lax.axis_index("col")
    x, core = row // 2, row % 2
    y, z = col // RING, col % RING
    half = z // 2
    inside = core == half
    pair = half * 2 + (z + 1) % 2
    cross = RING - 1 - z
    cz = jnp.where(inside, z, cross)
    work_row = x * 2 + half

    def when_in(f):
        pl.when(inside)(f)

    def when_out(f):
        pl.when(jnp.logical_not(inside))(f)

    def yz(dy, dz):
        return ((y + dy) % RING) * RING + (z + dz) % RING

    def at(dy, zz):
        return ((y + dy) % RING) * RING + zz

    def xrow(dx):
        return ((x + dx) % RING) * 2 + core

    sibling = x * 2 + 1 - core

    for s in range(SECTIONS):
        a_raw[s][A_SLOTS] = jnp.zeros((TILE, TILE), jnp.bfloat16)
        p_raw[s][P_SLOTS] = jnp.zeros((TILE, TILE), jnp.bfloat16)
    rounded[BR] = jnp.zeros((WIDE, TILE, TILE), jnp.bfloat16)

    barrier = pltpu.get_barrier_semaphore()
    peers = [{"col": yz(dy, dz)} for dy, dz in ORDER]
    peers += [{"row": sibling, "col": yz(dy, dz)} for dy, dz in ((0, 0),) + ORDER]
    peers += [{"row": xrow(dx)} for dx in SIDES]
    for peer in peers:
        pl.semaphore_signal(barrier, inc=1, device_id=peer, device_id_type=MESH)
    pl.semaphore_wait(barrier, len(peers))

    def remote(src, dst, peer, i, j=None):
        return pltpu.make_async_remote_copy(
            src_ref=src, dst_ref=dst, send_sem=ssem.at[i], recv_sem=rsem.at[i if j is None else j],
            device_id=peer, device_id_type=MESH,
        )

    def a_at(s, dy, zz, lo, n):
        return a_raw[s].at[pl.ds(at(dy, zz) * KA + lo, n)]

    def b_at(s, dy, lo, n):
        start = jnp.where(inside, at(dy, z) * KA + HALF, RELAY + ((y + dy) % RING) * HALF)
        return a_raw[s].at[pl.ds(start + lo, n)]

    def origin(j):
        return (z, pair, cross, RING - 1 - pair)[j]

    def p_at(s, xx, j):
        return p_raw[s].at[pl.ds((xx * 2 + j) * 2 * PJ, 2 * PJ)]

    def msg(s, *key):
        i = IDS[(s,) + key]
        kind = key[0]
        own = a_ref.at[s, pl.ds(HALF, HALF)]
        own_a = a_ref.at[s, pl.ds(0, HALF)]
        if kind == "by":
            return remote(own, b_at(s, 0, 0, HALF), {"col": yz(key[1], 0)}, i)
        if kind == "bf":
            part = b_at(s, -key[1], 0 if key[1] == 1 else QUARTER, QUARTER)
            return remote(part, part, {"col": yz(key[1], 0)}, i)
        if kind == "a_in":
            return remote(own_a, a_at(s, 0, z, 0, HALF), {"col": at(0, pair)}, i)
        if kind == "a_cr":
            return remote(own_a, a_at(s, 0, z, 0, HALF), {"col": at(0, cross)}, i)
        if kind == "a_cf":
            part = a_at(s, 0, cross, 0, HALF)
            return remote(part, part, {"col": at(0, pair)}, i)
        if kind in ("b_in", "b_cr"):
            dy, lo, n = PIECE[key[1]]
            src = own if dy == 0 else b_at(s, dy, lo, n)
            return remote(src, a_at(s, dy, z, HALF + lo, n), {"col": at(0, pair if kind == "b_in" else cross)}, i)
        if kind == "b_cf":
            dy, lo, n = PIECE[key[1]]
            part = a_at(s, dy, cross, HALF + lo, n)
            return remote(part, part, {"col": at(0, pair)}, i)
        if kind == "ay":
            part = a_at(s, 0, origin(key[1]), 0, HALF)
            return remote(own_a if key[1] == 0 else part, part, {"col": yz(key[2], 0)}, i)
        if kind == "af":
            part = a_at(s, -key[2], origin(key[1]), 0 if key[2] == 1 else QUARTER, QUARTER)
            return remote(part, part, {"col": yz(key[2], 0)}, i)
        if kind == "share":
            part = a_raw[s].at[pl.ds(at(key[1], 0) * KA, RING * KA)]
            return remote(part, part, {"row": sibling}, i)
        if kind == "p_own":
            return remote(p_ref.at[s], p_at(s, x, core), {"row": sibling}, i)
        if kind == "p_cr":
            mine = IDS[s, "p_cr", 0] + core
            return remote(p_ref.at[s], p_at(s, x, core), {"row": work_row, "col": at(0, cross)}, mine, mine if key[1] < 0 else i)
        if kind == "px":
            part = p_at(s, x, key[1])
            return remote(part, part, {"row": xrow(key[2])}, i)
        part = p_at(s, (x - key[1]) % RING, 0 if key[1] == 1 else 1)
        return remote(part, part, {"row": xrow(key[1])}, i)

    def start(s, *key):
        msg(s, *key).start()

    def wait(s, *key):
        msg(s, *key).wait_recv()

    def kept_a(s):
        return pltpu.make_async_copy(a_ref.at[s], a_at(s, 0, z, 0, KA), lsem.at[2 * s])

    def kept_p(s):
        return pltpu.make_async_copy(p_ref.at[s], p_at(s, x, core), lsem.at[2 * s + 1])

    def own(s):
        for n in SIDES:
            start(s, "by", n)

        @when_in
        def _():
            start(s, "a_in")
            for n in SIDES:
                start(s, "ay", 0, n)
            start(s, "b_in", 0)
            kept_a(s).start()

        @when_out
        def _():
            start(s, "a_cr")
            start(s, "b_cr", 0)

    def p_own(s):
        i = IDS[s, "p_cr", 0]
        cr = remote(p_ref.at[s], p_at(s, x, core), {"row": work_row, "col": at(0, cross)}, i + core, i + core)
        cr.start()

        @when_in
        def _():
            kept_p(s).start()

        @when_out
        def _():
            start(s, "p_own")

    def p_ring(s):
        for j in (0, 1):
            for n in SIDES:
                start(s, "px", j, n)

    def p_ring_in(s):
        @when_in
        def _():
            kept_p(s).wait()
            wait(s, "p_own")
            p_ring(s)

    def p_ring_out(s):
        @when_out
        def _():
            wait(s, "p_cr", 0)
            wait(s, "p_cr", 1)
            p_ring(s)

    def p_pass(s):
        wait(s, "px", 0, 1)
        start(s, "pf", 1)
        wait(s, "px", 1, 3)
        start(s, "pf", 3)

    def p_end(s):
        wait(s, "px", 1, 1)
        wait(s, "px", 0, 3)
        for n in SIDES:
            wait(s, "pf", n)

    def ring1(s):
        for n in SIDES:
            wait(s, "by", n)
            start(s, "bf", n)

        @when_in
        def _():
            start(s, "b_in", 2)
            start(s, "b_in", 1)

        @when_out
        def _():
            start(s, "b_cr", 2)
            start(s, "b_cr", 1)

    def ring2(s):
        for i, n in ((3, 1), (4, 3)):
            wait(s, "bf", n)

            @when_in
            def _():
                start(s, "b_in", i)

            @when_out
            def _():
                start(s, "b_cr", i)

    def alpha1(s):
        @when_in
        def _():
            wait(s, "a_cr")
            start(s, "a_cf")
            for n in SIDES:
                start(s, "ay", 2, n)
            wait(s, "a_in")
            for n in SIDES:
                start(s, "ay", 1, n)

    def alpha2(s):
        @when_in
        def _():
            wait(s, "a_cf")
            for n in SIDES:
                start(s, "ay", 3, n)

    def crossed(s, pieces):
        @when_in
        def _():
            for i in pieces:
                wait(s, "b_cr", i)
                start(s, "b_cf", i)

    def alpha3(s, origins):
        @when_in
        def _():
            for j in origins:
                for n in SIDES:
                    wait(s, "ay", j, n)
                    start(s, "af", j, n)

    def share(s, dy):
        @when_in
        def _():
            for i, (at_dy, _, _) in enumerate(PIECE):
                if at_dy == dy:
                    wait(s, "b_in", i)
                    wait(s, "b_cf", i)
            if dy == 0:
                kept_a(s).wait()
            if dy == 2:
                for j in range(4):
                    for n in SIDES:
                        wait(s, "af", j, n)
            start(s, "share", dy)

    def shared(s):
        @when_out
        def _():
            for dy in range(4):
                wait(s, "share", dy)

    def find():
        def iota(shape, dim):
            return lax.broadcasted_iota(jnp.int32, shape, dim)

        def column(line):
            n = line.shape[1]
            return jnp.sum(jnp.where(iota((n, n), 0) == iota((n, n), 1), line, 0), axis=1, keepdims=True)

        spots = iota((N_COL, BR * BK), 1)
        first = iota((N_COL, BR * BK), 0) * KA
        for s in range(SECTIONS):
            codes = a_rows[s] * BK + a_cols[s]
            best = jnp.full((N_COL, BR * BK), A_SLOTS, jnp.int32)
            for t in range(KA):
                best = jnp.minimum(best, jnp.where(column(codes[t : t + 1]) == spots, first + t, A_SLOTS))
            found[0, s : s + 1, :] = jnp.min(best, axis=0, keepdims=True)
        n_row = BK // 2
        spots = iota((n_row, BK * BC), 1)
        group = iota((n_row, BK * BC), 0)
        for s in range(SECTIONS):
            best = jnp.full((n_row, BK * BC), P_SLOTS, jnp.int32)
            for m in range(2):
                cols = p_cols[s, m]
                k = group * 2 + m
                for j in range(PJ):
                    best = jnp.minimum(best, jnp.where(k * BC + column(cols[j : j + 1]) == spots, k * PJ + j, P_SLOTS))
            found[1, s : s + 1, : BK * BC] = jnp.min(best, axis=0, keepdims=True)
        line = iota((BR, TILE), 0)
        spots = iota((BR, TILE), 1)
        named = column(owners[...]) == spots // MOST
        low = jnp.min(jnp.where(named, line, BR), axis=0, keepdims=True)
        high = jnp.max(jnp.where(named, line, -1), axis=0, keepdims=True)
        second = jnp.where(high > low, high, BR)
        slot = iota((1, TILE), 1) % MOST
        found[0, SECTIONS : SECTIONS + 1, :TILE] = jnp.where(slot == 0, low, second)

    def table_msgs():
        return (
            remote(found.at[0], taken.at[0], {"col": at(0, cross)}, TABLE_IDS),
            remote(found.at[1], taken.at[1], {"row": sibling}, TABLE_IDS + 1),
            remote(found, taken, {"row": sibling, "col": at(0, cross)}, TABLE_IDS + 2),
        )

    def find_tables():
        @when_out
        def _():
            find()
            for copy in table_msgs():
                copy.start()

    def take_tables():
        @when_in
        def _():
            for copy in table_msgs()[:2]:
                copy.wait_recv()

        @when_out
        def _():
            table_msgs()[2].wait_recv()

        copy = pltpu.make_async_copy(taken, tbl, tsem)
        copy.start()
        copy.wait()

    def place_p(s):
        @pl.loop(0, BK)
        def _(k):
            for c in range(BC):
                p_dense[pl.ds(pl.multiple_of(k * TILE, TILE), TILE), c * TILE : (c + 1) * TILE] = p_raw[s][
                    tbl[1, s, k * BC + c]
                ]

    def place_a(s):
        @pl.loop(0, BR)
        def _(r):
            for k in range(BK):
                a_dense[pl.ds(pl.multiple_of(r * TILE, TILE), TILE), k * TILE : (k + 1) * TILE] = a_raw[s][
                    tbl[0, s, r * BK + k]
                ]

    def part_dot(mb, nb):
        rows = pl.ds(pl.multiple_of(mb * MB, MB), MB)
        return jnp.dot(
            a_dense[rows, :], p_dense[:, nb * WIDE * TILE : (nb + 1) * WIDE * TILE], preferred_element_type=jnp.float32
        )

    def dots(s, nb):
        @pl.loop(0, BR * TILE // MB)
        def _(mb):
            rows = pl.ds(pl.multiple_of(mb * MB, MB), MB)
            value = part_dot(mb, nb)
            if s == 0:
                acc[nb, rows, :] = value
            else:
                acc[nb, rows, :] += value

    def finish(nb):
        @pl.loop(0, BR * TILE // MB)
        def _(mb):
            rows = pl.ds(pl.multiple_of(mb * MB, MB), MB)
            value = (acc[nb, rows, :] + part_dot(mb, nb)).astype(jnp.bfloat16)
            for i in range(MB // TILE):
                for j in range(WIDE):
                    rounded[mb * (MB // TILE) + i, j] = value[i * TILE : (i + 1) * TILE, j * TILE : (j + 1) * TILE]

        @pl.loop(0, N_COL)
        def _(o):
            for q in range(MOST):
                staged[nb, o, q] = rounded[tbl[0, SECTIONS, o * MOST + q]]

        @when_in
        def _():
            out_own(nb).start()

        @when_out
        def _():
            out_msg(nb, 0, 0).start()

        for dy, dz in out_order():
            out_msg(nb, dy, dz).start()

    def out_at(nb, c):
        return out_ref.at[:, pl.ds(c * BC + nb * WIDE, WIDE)]

    def out_own(nb):
        return pltpu.make_async_copy(staged.at[nb, col], out_at(nb, col), lsem.at[2 * SECTIONS + nb])

    def out_msg(nb, dy, dz):
        base = OUT_IDS + nb * N_COL
        c = at(0, cz)
        o = yz(dy, dz)
        return remote(staged.at[nb, o], out_at(nb, c), {"row": work_row, "col": o}, base + o, base + c)

    def out_wait(nb):
        @pl.loop(0, N_COL)
        def _(c):
            @pl.when(jnp.logical_not(inside & (c == col)))
            def _():
                i = OUT_IDS + nb * N_COL + c
                remote(staged.at[nb, c], out_at(nb, c), {"row": sibling}, i, i).wait_recv()

    def sent():
        for s in range(SECTIONS):
            i = IDS[s, "p_cr", 0] + core
            remote(p_ref.at[s], p_at(s, x, core), {"row": work_row, "col": at(0, cross)}, i, i).wait_send()
            for key in KEYS:
                if key[0] in ("by", "bf", "px", "pf"):
                    msg(s, *key).wait_send()

        @when_in
        def _():
            for s in range(SECTIONS):
                for key in KEYS:
                    if key[0] in ("a_in", "a_cf", "b_in", "b_cf", "ay", "af", "share"):
                        msg(s, *key).wait_send()

        @when_out
        def _():
            for s in range(SECTIONS):
                for key in KEYS:
                    if key[0] in ("a_cr", "b_cr", "p_own"):
                        msg(s, *key).wait_send()
            for copy in table_msgs():
                copy.wait_send()

    def out_order():
        for (dy, dz), (oy, oz) in zip(ORDER, ORDER[TURN:] + ORDER[:TURN]):
            yield jnp.where(inside, dy, oy), jnp.where(inside, dz, oz)

    def out_sent(nb):
        @when_in
        def _():
            out_own(nb).wait()

        @when_out
        def _():
            out_msg(nb, 0, 0).wait_send()

        for dy, dz in ORDER:
            out_msg(nb, dy, dz).wait_send()

    def moves(s):
        return [
            lambda: ring1(s),
            lambda: alpha1(s),
            lambda: p_ring_out(s),
            lambda: ring2(s),
            lambda: alpha2(s),
            lambda: crossed(s, (0, 1, 2)),
            lambda: p_pass(s),
            lambda: alpha3(s, (0,)),
            lambda: crossed(s, (3, 4)),
            lambda: alpha3(s, (2, 1)),
            lambda: share(s, 0),
            lambda: alpha3(s, (3,)),
            lambda: share(s, 1),
            lambda: share(s, 3),
            lambda: share(s, 2),
        ]

    def work(s):
        def first():
            p_end(s)
            place_p(s)
            shared(s)
            place_a(s)

        return [first] + [lambda nb=nb: dots(s, nb) for nb in range(1)]

    def mix(many, few):
        done = 0
        for i, f in enumerate(many):
            f()
            while done * len(many) < (i + 1) * len(few):
                few[done]()
                done += 1

    for step in plan(own, p_own, p_ring_in, find_tables, take_tables, moves, work):
        step()
    work(2)[0]()
    finish(0)
    for chunks in (range(1, 2), range(2, CHUNKS)):
        for s in range(SECTIONS):
            place_p(s)
            place_a(s)
            for nb in chunks:
                if s < SECTIONS - 1:
                    dots(s, nb)
                else:
                    finish(nb)
    sent()
    for nb in range(CHUNKS):
        out_sent(nb)
        out_wait(nb)


EARLY = 2
LAG = 3
TABLES = 8
AFTER = 15


def plan(own, p_own, p_ring_in, find_tables, take_tables, moves, work):
    steps = []
    for s in range(SECTIONS):
        if s < EARLY:
            steps += [functools.partial(own, s), functools.partial(p_own, s)]
        if s == 0:
            steps += [functools.partial(p_ring_in, 0)]
    timed = []
    for s in range(SECTIONS):
        for i, f in enumerate(moves(s)):
            timed.append((s * LAG + i, s, f))
        if s >= EARLY:
            timed.append((s * LAG - 3, s, functools.partial(own, s)))
            timed.append((s * LAG - 3, s, functools.partial(p_own, s)))
        if s:
            timed.append((s * LAG / 2 + 1 if s < EARLY else s * LAG - 2, s, functools.partial(p_ring_in, s)))
    timed.append((TABLES, 0, find_tables))
    timed.append((AFTER, 0, take_tables))
    for s in range(SECTIONS - 1):
        for i, f in enumerate(work(s)):
            timed.append((s * LAG + AFTER + i, 9, f))
    timed.sort(key=lambda t: t[:2])
    return steps + [f for _, _, f in timed]


def settle(held, out_ref, sems):
    n = N_COL * BC // PIECES
    copies = []
    for q in range(MOST):
        for i in range(PIECES):
            part = (q, pl.ds(i * n, n))
            copies.append(pltpu.make_async_copy(held.at[part], out_ref.at[part], sems.at[q * PIECES + i]))
            copies[-1].start()
    for copy in copies:
        copy.wait()


def body(a_tiles, a_rows, a_cols, p_tiles, p_cols, owners):
    a = a_tiles.reshape(SECTIONS, KA, TILE, TILE)
    p = p_tiles.reshape(SECTIONS, 2 * PJ, TILE, TILE)
    bf = jnp.bfloat16
    vmem = pl.BlockSpec(memory_space=pltpu.VMEM)
    hbm = pl.BlockSpec(memory_space=pl.ANY)
    shape = (MOST, N_COL * BC, TILE, TILE)
    held = pl.pallas_call(
        kernel,
        name="block_product",
        out_shape=pltpu.VMEM(shape, bf),
        in_specs=[vmem] * 4 + [hbm] * 2,
        out_specs=vmem,
        scratch_shapes=[pltpu.VMEM((RELAY + RING * HALF, TILE, TILE), bf)] * SECTIONS
        + [pltpu.VMEM((P_SLOTS + 1, TILE, TILE), bf)] * SECTIONS
        + [
            pltpu.VMEM((BR * TILE, BK * TILE), bf),
            pltpu.VMEM((BK * TILE, BC * TILE), bf),
            pltpu.VMEM((CHUNKS, BR * TILE, WIDE * TILE), jnp.float32),
            pltpu.VMEM((BR + 1, WIDE, TILE, TILE), bf),
            pltpu.VMEM((CHUNKS, N_COL, MOST, WIDE, TILE, TILE), bf),
            pltpu.VMEM((2, 8, BR * BK), jnp.int32),
            pltpu.VMEM((2, 8, BR * BK), jnp.int32),
            pltpu.SMEM((2, 8, BR * BK), jnp.int32),
            pltpu.SemaphoreType.DMA((N_COPIES,)),
            pltpu.SemaphoreType.DMA((N_COPIES,)),
            pltpu.SemaphoreType.DMA((2 * SECTIONS + CHUNKS,)),
            pltpu.SemaphoreType.DMA,
        ],
        compiler_params=pltpu.CompilerParams(collective_id=0, has_side_effects=True, vmem_limit_bytes=52 << 20),
        cost_estimate=pl.CostEstimate(flops=25_769_803_776, bytes_accessed=20_000_000, transcendentals=0),
    )(
        jnp.transpose(a_rows[0], (1, 2, 0)),
        jnp.transpose(a_cols[0], (1, 2, 0)),
        jnp.transpose(p_cols[:, :, :, 0], (1, 2, 3, 0)),
        owners.reshape(1, BR),
        a,
        p,
    )
    return pl.pallas_call(
        settle,
        name="settle",
        out_shape=jax.ShapeDtypeStruct(shape, bf),
        in_specs=[vmem],
        out_specs=hbm,
        scratch_shapes=[pltpu.SemaphoreType.DMA((MOST * PIECES,))],
        compiler_params=pltpu.CompilerParams(vmem_limit_bytes=2 << 20),
    )(held)


def solution(mesh):
    placed = (
        P("row", "col", None, None, None, None),
        P("row", None, None, None),
        P("row", None, None, None),
        P("row", None, None, "col", None, None, None),
        P(None, None, None, "col", None),
        P("row", None),
    )
    return jax.shard_map(
        body,
        mesh=mesh,
        in_specs=placed,
        out_specs=P(("row", "col"), None, None, None),
        check_vma=False,
    )
```
